256 devices in a mesh: gx: 32 (over z, y), gy: 8 (over x, core).
Axes of the slice: x: 4, y: 4, z: 8, core: 2. Of those that a mesh axis runs over, the one named last changes fastest.
Arguments:
- positions: float32 [3, 1048576], P(None, ('gx', 'gy')), may hold values from 0 to 512, as said below
- mass: float32 [1048576], P(('gx', 'gy')), may hold values from 0.5 to 2
- smoothing: float32 [1048576], P(('gx', 'gy')), may hold values from 1.5 to 3
- energy: float32 [1048576], P(('gx', 'gy')), may hold values from 0.5 to 4
- destination: int32 [1048576, 1], P(('gx', 'gy')), may hold values from 0 to 255, as said below
- pairs: int32 [2, 221184], P(None, ('gx', 'gy')), may hold values from 0 to 63, as said below
- pair_count: int32 [256], P(('gx', 'gy')), may hold values from 432 to 864, as said below
Outputs:
- density: float32 [1048576], P(('gx', 'gy'))
- accel: float32 [3, 1048576], P(None, ('gx', 'gy'))
The draws below stay inside these ranges and needn't reach their ends.
Inputs may be any that keep to these rules, and one draw needn't show every extreme that they name: `destination`: the 4096 particles of every domain name each domain exactly 16 times. `positions`: each particle lies in the box of its new domain (i, j): first coordinate in [16 i, 16 (i + 1)], second in [16 j, 16 (j + 1)], third in [0, 16]. `pairs`: row 0 holds target tiles below 32, row 1 source tiles below 32 + 4 * 8 (tiles from 32 on are ghost tiles); domain d's list is columns d * 864 to (d + 1) * 864 - 1, and slots from pair_count[d] on are unused. `pair_count`: some domain uses all 864 slots.
All inputs are finite; a program needn't handle non-finite values.
Results may differ from the reference program's by a relative error of at most 0.0005.
Values sent between devices are 32-bit elements; how exact they have to be, the bound alone decides.
No kernel may reach another device: no remote copies, remote signals or barrier semaphores. Data moves between devices by JAX's collectives and lax.ppermute only.
A program may use at most 64 MiB of HBM per device.

```python
import math
import jax
import jax.numpy as jnp
from jax import lax

P_DEV = 4096
TILE = 128
GT = 8
BOX = 16
NPART = 1048576
CAP = 16
NT = 32
MAXP = 864
DEPTH = 16
N_GX = 32
N_GY = 8
DEVICES = 256


def route_plan(key):
    keys = jax.random.split(jax.random.fold_in(key, 31), DEVICES)
    base = jnp.repeat(jnp.arange(DEVICES, dtype=jnp.int32), CAP)
    return jax.vmap(lambda one: jax.random.permutation(one, base))(keys).astype(jnp.int32)


def draw_destination(key, part):
    return route_plan(key).reshape(-1, 1)


def draw_positions(key, part):
    plan = route_plan(key)
    order = jnp.argsort(plan, axis=1, stable=True).astype(jnp.int32)
    placed = jnp.argsort(order, axis=1, stable=True).astype(jnp.int32)
    source = jnp.arange(DEVICES, dtype=jnp.int32)[:, None]
    column = source * CAP + placed - plan * CAP
    edge = column < GT * TILE
    first = (plan // N_GY).astype(jnp.float32)
    second = (plan % N_GY).astype(jnp.float32)
    spread = jax.random.uniform(jax.random.fold_in(key, 41), (3, DEVICES, P_DEV), jnp.float32)
    coord_x = (first + spread[0]) * BOX
    coord_y = (second + spread[1]) * BOX
    coord_z = spread[2] * DEPTH
    face = jax.random.randint(jax.random.fold_in(key, 42), (DEVICES, P_DEV), 0, 4)
    near = jax.random.uniform(jax.random.fold_in(key, 43), (DEVICES, P_DEV), jnp.float32) * 3.0
    coord_x = jnp.where(edge & (face == 0), first * BOX + near, coord_x)
    coord_x = jnp.where(edge & (face == 1), (first + 1.0) * BOX - near, coord_x)
    coord_y = jnp.where(edge & (face == 2), second * BOX + near, coord_y)
    coord_y = jnp.where(edge & (face == 3), (second + 1.0) * BOX - near, coord_y)
    return jnp.stack([coord_x, coord_y, coord_z]).reshape(3, -1).astype(jnp.float32)


def draw_pairs(key, part):
    total = DEVICES * MAXP
    target = jax.random.randint(jax.random.fold_in(key, 11), (total,), 0, NT)
    source = jax.random.randint(jax.random.fold_in(key, 12), (total,), 0, NT + 4 * GT)
    return jnp.stack([target, source]).astype(jnp.int32)


def draw_pair_count(key, part):
    counts = jax.random.randint(jax.random.fold_in(key, 21), (DEVICES,), MAXP // 2, MAXP + 1)
    fullest = jax.random.randint(jax.random.fold_in(key, 22), (), 0, DEVICES)
    return jnp.where(jnp.arange(DEVICES) == fullest, MAXP, counts).astype(jnp.int32)


def shard_levels(own_key, shape, pieces, low, top_value):
    factor_of = 1.0
    for position, blocks in pieces:
        steps = jax.random.uniform(jax.random.fold_in(jax.random.fold_in(own_key, 6), position), (blocks,), jnp.float32, low / len(pieces), top_value / len(pieces))
        factor_of = factor_of * jnp.repeat(jnp.exp(steps), shape[position] // blocks).reshape((-1,) + (1,) * (len(shape) - 1 - position))
    return factor_of


def setup_inputs(seed: int = 0) -> dict:
    streams_of = jax.random.split(jax.random.key(seed), 8)
    positions = draw_positions(jax.random.fold_in(streams_of[7], 71), 0)
    mass = jnp.clip(jnp.exp(math.log(2.0) - 1.3862944 * jax.random.uniform(streams_of[1], (NPART,), jnp.float32) ** shard_levels(streams_of[1], (NPART,), ((0, 256),), -0.2, 0.2)), 0.5, 2.0)
    smoothing = jnp.clip(1.5 + 1.5 * jax.random.uniform(streams_of[2], (NPART,), jnp.float32) ** shard_levels(streams_of[2], (NPART,), ((0, 256),), -0.2, 0.2), 1.5, 3.0)
    energy = jnp.clip(jnp.exp(math.log(4.0) - 2.0794415 * jax.random.uniform(streams_of[3], (NPART,), jnp.float32) ** shard_levels(streams_of[3], (NPART,), ((0, 256),), -0.2, 0.2)), 0.5, 4.0)
    destination = draw_destination(jax.random.fold_in(streams_of[7], 71), 0)
    pairs = draw_pairs(jax.random.fold_in(streams_of[7], 71), 0)
    pair_count = draw_pair_count(jax.random.fold_in(streams_of[7], 71), 0)
    return {"positions": positions, "mass": mass, "smoothing": smoothing, "energy": energy, "destination": destination, "pairs": pairs, "pair_count": pair_count}


KERNEL_NORM = 21.0 / (2.0 * math.pi)
GAMMA_LESS = 2.0 / 3.0

def neighbour_rows(boundary):
    padded = jnp.pad(boundary, ((0, 0), (1, 1), (1, 1), (0, 0)))
    return jnp.concatenate([padded[:, :-2, 1:-1], padded[:, 2:, 1:-1], padded[:, 1:-1, :-2], padded[:, 1:-1, 2:]], axis=3)

def density_domain(pool, pair_list, count, own_tiles):
    slots = pair_list.shape[1]
    group_size = slots // own_tiles
    tile_rows = pool.shape[2]

    def advance(totals, block):
        start = block * group_size
        target = lax.dynamic_slice_in_dim(pair_list[0], start, group_size)
        source = lax.dynamic_slice_in_dim(pair_list[1], start, group_size)
        active = start + jnp.arange(group_size, dtype=jnp.int32) < count
        nearer = pool[target]
        farther = pool[source]
        dist_sq = jnp.zeros((group_size, tile_rows, tile_rows), jnp.float32)
        for component in range(3):
            offset = nearer[:, component, :, None] - farther[:, component, None, :]
            dist_sq = dist_sq + offset * offset
        radius = nearer[:, 4, :, None]
        ratio = jnp.sqrt(dist_sq) / radius
        falloff = jnp.maximum(1.0 - ratio, 0.0)
        kernel = KERNEL_NORM / (radius * radius * radius) * falloff ** 4 * (1.0 + 4.0 * ratio)
        summed = lax.optimization_barrier(jnp.sum(kernel * farther[:, 3, None, :], axis=2))
        summed = jnp.where(active[:, None], summed, 0.0)
        return (totals.at[target].add(summed), None)
    start_totals = jnp.zeros((own_tiles, tile_rows), jnp.float32)
    totals, unused = lax.scan(advance, start_totals, jnp.arange(slots // group_size, dtype=jnp.int32))
    own = pool[:own_tiles]
    radius = own[:, 4, :]
    self_term = own[:, 3, :] * KERNEL_NORM / (radius * radius * radius)
    return (totals + self_term).reshape(-1)

def accel_domain(pool, press_pool, pair_list, count, own_tiles):
    slots = pair_list.shape[1]
    group_size = slots // own_tiles
    tile_rows = pool.shape[2]

    def advance(totals, block):
        start = block * group_size
        target = lax.dynamic_slice_in_dim(pair_list[0], start, group_size)
        source = lax.dynamic_slice_in_dim(pair_list[1], start, group_size)
        active = start + jnp.arange(group_size, dtype=jnp.int32) < count
        nearer = pool[target]
        farther = pool[source]
        press_own = press_pool[target]
        press_far = press_pool[source]
        dist_sq = jnp.zeros((group_size, tile_rows, tile_rows), jnp.float32)
        for component in range(3):
            offset = nearer[:, component, :, None] - farther[:, component, None, :]
            dist_sq = dist_sq + offset * offset
        mean_radius = 0.5 * (nearer[:, 4, :, None] + farther[:, 4, None, :])
        ratio = jnp.sqrt(dist_sq) / mean_radius
        falloff = jnp.maximum(1.0 - ratio, 0.0)
        slope = -20.0 * KERNEL_NORM * falloff ** 3 / mean_radius ** 5
        coupling = farther[:, 3, None, :] * (press_own[:, :, None] + press_far[:, None, :]) * slope
        summed = lax.optimization_barrier(jnp.sum(coupling, axis=2))
        parts_list = []
        for component in range(3):
            pulled = lax.optimization_barrier(jnp.sum(coupling * farther[:, component, None, :], axis=2))
            parts_list.append(-(nearer[:, component, :] * summed - pulled))
        result = jnp.stack(parts_list, axis=1)
        result = jnp.where(active[:, None, None], result, 0.0)
        return (totals.at[target].add(result), None)
    start_totals = jnp.zeros((own_tiles, 3, tile_rows), jnp.float32)
    totals, unused = lax.scan(advance, start_totals, jnp.arange(slots // group_size, dtype=jnp.int32))
    return jnp.transpose(totals, (1, 0, 2)).reshape(3, -1)

def reference(positions, mass, smoothing, energy, destination, pairs, pair_count):
    domains = N_GX * N_GY
    edge_rows = GT * TILE
    fields = jnp.concatenate([positions, mass[None], smoothing[None], energy[None]], 0).reshape(6, domains, P_DEV)
    ranking = jnp.argsort(destination[:, 0].reshape(domains, P_DEV), axis=1, stable=True).astype(jnp.int32)
    outgoing = jnp.take_along_axis(fields, ranking[None], axis=2).reshape(6, domains, domains, CAP)
    settled = jnp.transpose(outgoing, (0, 2, 1, 3)).reshape(6, domains, P_DEV)
    boundary = settled[:, :, :edge_rows].reshape(6, N_GX, N_GY, edge_rows)
    extra = neighbour_rows(boundary).reshape(6, domains, 4 * edge_rows)
    pool = jnp.concatenate([settled, extra], 2).reshape(6, domains, NT + 4 * GT, TILE)
    pool = jnp.transpose(pool, (1, 2, 0, 3))
    pair_lists = jnp.transpose(pairs.reshape(2, domains, MAXP), (1, 0, 2))
    density = lax.map(lambda items: density_domain(items[0], items[1], items[2], NT), (pool, pair_lists, pair_count))
    press = GAMMA_LESS * settled[5] / density
    press_edge = press[:, :edge_rows].reshape(1, N_GX, N_GY, edge_rows)
    press_extra = neighbour_rows(press_edge).reshape(domains, 4 * edge_rows)
    press_pool = jnp.concatenate([press, press_extra], 1).reshape(domains, NT + 4 * GT, TILE)
    accel = lax.map(lambda items: accel_domain(items[0], items[1], items[2], items[3], NT), (pool, press_pool, pair_lists, pair_count))
    accel = jnp.transpose(accel, (1, 0, 2)).reshape(3, -1)
    return (density.reshape(-1), accel)
```

```python
import functools
import math

import jax
import jax.numpy as jnp
from jax import lax
from jax.experimental import pallas as pl
from jax.experimental.pallas import tpu as pltpu
from jax.sharding import PartitionSpec as P

F32, BF16, I32 = jnp.float32, jnp.bfloat16, jnp.int32
TILE = 128
OWN = 32
GT = 8
ALL = OWN + 4 * GT
CAP = 16
BOX = 16.0
HALF = 8.0
KEYS = 48
GROUP = 2
KERNEL_NORM = 21.0 / (2.0 * math.pi)
GAMMA_LESS = 2.0 / 3.0
STARTS = (0, 1024, 1280, 2048)

NT = (((1,), (1,)), ((), ()))
NN = (((1,), (0,)), ((), ()))


def iota(shape, axis):
    return lax.broadcasted_iota(I32, shape, axis)


def dot(a, b, dims=NN):
    return lax.dot_general(a, b, dims, preferred_element_type=F32)


def pieces(v):
    one = v.astype(BF16).astype(F32)
    rest = v - one
    two = rest.astype(BF16).astype(F32)
    return one, two, rest - two


def dispatch_kernel(pos, mass, smooth, energy, dest, out):
    width = 256
    n = pos.shape[1]
    row = iota((width, width), 0)
    upper = (row < iota((width, width), 1)).astype(F32).astype(BF16)
    ones = jnp.ones((width, width), BF16)
    carry = jnp.zeros((width, width), F32)
    total = jnp.zeros((width, 128), F32)
    ranks = iota((CAP, width), 0)
    for b in range(n // width):
        at = slice(b * width, (b + 1) * width)
        mine = row == dest[:, at]
        hot = jnp.where(mine, 1.0, 0.0)
        hot16 = hot.astype(BF16)
        before = dot(hot16, upper) + carry
        carry = carry + dot(hot16, ones)
        rank = jnp.sum(hot * before, axis=0, keepdims=True).astype(I32)
        sel = ranks == rank
        rows = [pos[0:1, at], pos[1:2, at], pos[2:3, at], mass[:, at], smooth[:, at], energy[:, at]]
        spread = jnp.concatenate(
            [jnp.where(sel, v, 0.0) for v in rows] + [jnp.zeros((2 * CAP, width), F32)], axis=0
        )
        for piece in pieces(spread):
            total = total + dot(hot16, piece.astype(BF16), NT)
    out[...] = total


def list_kernel(count, pairs, out):
    slots = pairs.shape[1]
    target, source = pairs[0:1, :], pairs[1:2, :]
    ghost = (source >= OWN).astype(I32)
    line = jnp.where(iota((1, slots), 1) < count[0], target + OWN * ghost, -1)
    column = source - OWN * ghost
    lines = jnp.where(iota((ALL, slots), 0) == line, 1.0, 0.0).astype(BF16)
    columns = jnp.where(iota((OWN, slots), 0) == column, 1.0, 0.0).astype(BF16)
    times = dot(columns, lines, NT)
    has = jnp.where(times > 0.0, 1.0, 0.0)
    has16 = has.astype(BF16)
    lower = jnp.where(iota((OWN, OWN), 0) > iota((OWN, OWN), 1), 1.0, 0.0).astype(BF16)
    within = dot(lower, has16)
    per_line = dot(jnp.ones((OWN, OWN), BF16), has16)
    la, lb = iota((ALL, ALL), 0), iota((ALL, ALL), 1)

    def section(k):
        return (k >= OWN).astype(I32) + (k >= OWN + GT).astype(I32)

    ahead = jnp.where((la < lb) & (section(la) == section(lb)), 1.0, 0.0).astype(BF16)
    lane = iota((OWN, ALL), 1)
    start = jnp.where(lane < OWN, STARTS[0], jnp.where(lane < OWN + GT, STARTS[1], STARTS[2]))
    place = within + dot(per_line.astype(BF16), ahead) + start.astype(F32)
    high = jnp.floor(place * (1.0 / 128.0))
    low = (place - 128.0 * high).astype(I32)
    high = jnp.where(has > 0.0, high.astype(I32), -1)
    sub = iota((OWN, ALL), 0)
    code = times * 2048.0 + ((lane % OWN) * 64 + sub + jnp.where(lane >= OWN, OWN, 0)).astype(F32)
    total = jnp.zeros((48, 128), F32)
    parts = pieces(code)
    for k in range(OWN):
        picked = iota((16, ALL), 0) == high[k : k + 1]
        left = jnp.concatenate([jnp.where(picked, p[k : k + 1], 0.0) for p in parts], axis=0)
        right = jnp.where(iota((128, ALL), 0) == low[k : k + 1], 1.0, 0.0)
        total = total + dot(left.astype(BF16), right.astype(BF16), NT)
    out[0:16] = (total[0:16] + total[16:32] + total[32:48]).astype(I32)
    lane1 = iota((1, ALL), 1)
    tallies = []
    for k in range(3):
        tallies.append(jnp.sum(jnp.where(section(lane1) == k, per_line[0:1], 0.0), axis=1, keepdims=True))
    r = iota((8, 128), 0)
    counts = jnp.where(r == 0, tallies[0], jnp.where(r == 1, tallies[1], tallies[2]))
    out[16:24] = counts.astype(I32)


def fields_of(block, shift):
    sub, lane = iota((8, 128), 0), iota((8, 128), 1) // CAP
    for bit in (1, 2, 4):
        up = pltpu.roll(pltpu.roll(block, bit, 0), 128 - CAP * bit, 1)
        down = up if bit == 4 else pltpu.roll(pltpu.roll(block, 8 - bit, 0), CAP * bit, 1)
        i, j = (sub // bit) % 2, (lane // bit) % 2
        block = jnp.where(i == j, block, jnp.where(i == 1, up, down))
    block = block - shift
    square = jnp.sum(jnp.where(sub < 3, block * block, 0.0), axis=0, keepdims=True)
    return jnp.where(sub == 6, square, jnp.where(sub == 7, 1.0, block))


def source_factor(v):
    a, b, c = pieces(v)
    return jnp.concatenate([a, a, a, b, b, c], axis=0)


def target_factor(u):
    a, b, c = pieces(u)
    return jnp.concatenate([a, b, c, a, b, a], axis=0)


def coefficients(v):
    sub = iota((8, 128), 0)
    return jnp.where(sub < 3, -2.0 * v, jnp.where(sub == 6, 1.0, jnp.where(sub == 7, v[6:7], 0.0)))


def entry(codes, e):
    code = codes[e >> 7, e & 127]
    return (code >> 6) & (OWN - 1), code & (ALL - 1), code >> 11


def sweep(codes, section, product, process, buffers):
    start = STARTS[section]
    last = STARTS[section + 1] - 1
    count = codes[16 + section, 0]

    def load(group, buffer):
        for k in range(GROUP):
            t, s, _ = entry(codes, jnp.minimum(start + group * GROUP + k, last))
            buffer[k] = product(t, s)

    def work(group, buffer):
        for k in range(GROUP):
            e = start + group * GROUP + k
            t, s, times = entry(codes, jnp.minimum(e, last))
            process(t, s, jnp.where(e < start + count, times, 0), buffer, k)

    load(0, buffers[0])

    def body(i, unused):
        load(2 * i + 1, buffers[1])
        work(2 * i, buffers[0])
        load(2 * i + 2, buffers[0])
        work(2 * i + 1, buffers[1])
        return unused

    lax.fori_loop(0, (count + 2 * GROUP - 1) // (2 * GROUP), body, 0)


def density_kernel(codes, centre, moved, g0, g1, g2, g3, density, press, fields, factors, right, sums, buf0, buf1):
    sub = iota((8, 128), 0)
    shift = jnp.where(sub == 0, centre[0], jnp.where(sub == 1, centre[1], jnp.where(sub == 2, HALF, 0.0)))

    def place(tile, block):
        v = fields_of(block, shift)
        fields[tile] = v
        factors[tile] = jnp.transpose(source_factor(v)).astype(BF16)
        return v

    weigh = jnp.where(sub == 3, 4.0, 0.0)
    none = jnp.zeros((8, 128), F32)
    weigh = jnp.concatenate([weigh, none, none, weigh, none, weigh], axis=0).astype(BF16)

    def own(tile, unused):
        v = place(tile, moved[pl.ds(pl.multiple_of(tile * 8, 8), 8)])
        h = v[4:5]
        right[tile, :, 0:128] = target_factor(coefficients(v) * (1.0 / (h * h))).astype(BF16)
        right[tile, :, 128:256] = weigh
        sums[tile] = none
        return unused

    lax.fori_loop(0, OWN, own, 0)
    for k, ghost in enumerate((g0, g1, g2, g3)):

        def other(tile, unused):
            place(OWN + k * GT + tile, ghost[pl.ds(pl.multiple_of(tile * 8, 8), 8)])
            return unused

        lax.fori_loop(0, GT, other, 0)

    def product(t, s):
        return dot(factors[s], right[t])

    def process(t, s, times, buffer, k):
        ratio_sq = jnp.maximum(buffer[k, :, 0:128], 1e-30)
        ratio = ratio_sq * lax.rsqrt(ratio_sq)
        falloff = jnp.maximum(1.0 - ratio, 0.0)
        falloff = falloff * falloff
        falloff = falloff * falloff
        term = falloff * (ratio + 0.25) * buffer[k, :, 128:256]
        sums[t] += jnp.sum(term.reshape(16, 8, 128), axis=0) * jnp.full((8, 128), times, I32).astype(F32)

    for section in range(3):
        sweep(codes, section, product, process, (buf0, buf1))
    total = jnp.sum(sums[...], axis=1)
    h = fields[0:OWN, 4, :]
    result = KERNEL_NORM / (h * h * h) * (total + fields[0:OWN, 3, :])
    density[...] = result
    press[...] = GAMMA_LESS * fields[0:OWN, 5, :] / result


def accel_kernel(codes, fields, factors, press, p0, p1, p2, p3, accel, right, pulls, sums, buf0, buf1):
    sub = iota((8, 128), 0)
    none = jnp.zeros((8, 128), F32)

    def pull(tile, p):
        v = fields[tile]
        x = jnp.where(sub < 4, pltpu.roll(v, 1, 0), pltpu.roll(v, 5, 0))
        x = jnp.where(sub % 4 == 0, 1.0, x) * v[3:4]
        x = jnp.where(sub < 4, x, x * p)
        both = jnp.concatenate([*pieces(x), none], axis=0).astype(BF16)
        pulls[tile, :, 0:128] = both
        pulls[tile, :, 128:256] = both
        return v

    def own(tile, unused):
        v = pull(tile, press[pl.ds(tile, 1)])
        right[tile, :, 0:128] = target_factor(coefficients(v)).astype(BF16)
        h = jnp.where(sub == 4, 1.0, jnp.where(sub == 7, v[4:5], 0.0))
        right[tile, :, 128:256] = target_factor(h).astype(BF16)
        sums[tile] = jnp.zeros((32, 128), F32)
        return unused

    lax.fori_loop(0, OWN, own, 0)
    for k, ghost in enumerate((p0, p1, p2, p3)):

        def other(tile, unused):
            pull(OWN + k * GT + tile, ghost[pl.ds(tile, 1)])
            return unused

        lax.fori_loop(0, GT, other, 0)

    def product(t, s):
        return dot(factors[s], right[t])

    def process(t, s, times, buffer, k):
        dist_sq = jnp.maximum(buffer[k, :, 0:128], 1e-30)
        near = 1.0 / buffer[k, :, 128:256]
        near_sq = near * near
        gap = jnp.maximum(near - dist_sq * lax.rsqrt(dist_sq) * (2.0 * near_sq), 0.0)
        slope = gap * gap * gap * near_sq
        first = slope.astype(BF16)
        second = (slope - first.astype(F32)).astype(BF16)
        both = jnp.concatenate([first, second], axis=0)
        sums[t] += dot(pulls[s], both) * jnp.full((32, 128), times, I32).astype(F32)

    for section in range(3):
        sweep(codes, section, product, process, (buf0, buf1))

    def finish(tile, unused):
        v = fields[tile]
        s = sums[tile]
        s = s[0:8] + s[8:16] + s[16:24]
        p = press[pl.ds(tile, 1)]
        a = p * (v * s[0:1] - pltpu.roll(s, 7, 0)) + (v * s[4:5] - pltpu.roll(s, 3, 0))
        accel[:, pl.ds(pl.multiple_of(tile * 128, 128), 128)] = a[0:3] * (640.0 * KERNEL_NORM)
        return unused

    lax.fori_loop(0, OWN, finish, 0)


def call(kernel, shapes, scratch=(), smem=0, args=(), limit=40):
    specs = [pl.BlockSpec(memory_space=pltpu.SMEM)] * smem
    specs += [pl.BlockSpec(memory_space=pltpu.VMEM)] * (len(args) - smem)
    return pl.pallas_call(
        kernel,
        out_shape=[jax.ShapeDtypeStruct(s, d) for s, d in shapes],
        in_specs=specs,
        out_specs=[pl.BlockSpec(memory_space=pltpu.VMEM)] * len(shapes),
        scratch_shapes=list(scratch),
        compiler_params=pltpu.CompilerParams(vmem_limit_bytes=limit * 2**20),
    )(*args)


def around(edge):
    taken = []
    for axis in ("gx", "gy"):
        count = lax.axis_size(axis)
        forward = [(i, i + 1) for i in range(count - 1)]
        taken.append(lax.ppermute(edge, axis, forward))
        taken.append(lax.ppermute(edge, axis, [(b, a) for a, b in forward]))
    return taken


def local(positions, mass, smoothing, energy, destination, pairs, pair_count):
    rows = mass.shape[0]
    flat = [a.reshape(1, rows) for a in (mass, smoothing, energy, destination)]
    (outgoing,) = call(dispatch_kernel, [((256, 128), F32)], args=(positions, *flat))
    (codes,) = call(list_kernel, [((24, 128), I32)], smem=1, args=(pair_count, pairs))
    moved = lax.all_to_all(outgoing, ("gx", "gy"), split_axis=0, concat_axis=0, tiled=True)
    ghosts = around(moved[: GT * 8])
    centre = jnp.stack([lax.axis_index("gx"), lax.axis_index("gy")]).astype(F32) * BOX + HALF
    density, press, fields, factors = call(
        density_kernel,
        [((OWN, 128), F32), ((OWN, 128), F32), ((ALL, 8, 128), F32), ((ALL, 128, KEYS), BF16)],
        scratch=[
            pltpu.VMEM((OWN, KEYS, 256), BF16),
            pltpu.VMEM((OWN, 8, 128), F32),
            pltpu.VMEM((GROUP, 128, 256), F32),
            pltpu.VMEM((GROUP, 128, 256), F32),
        ],
        smem=2,
        args=(codes, centre, moved, *ghosts),
    )
    presses = around(press[:GT])
    (accel,) = call(
        accel_kernel,
        [((3, rows), F32)],
        scratch=[
            pltpu.VMEM((OWN, KEYS, 256), BF16),
            pltpu.VMEM((ALL, 32, 256), BF16),
            pltpu.VMEM((OWN, 32, 128), F32),
            pltpu.VMEM((GROUP, 128, 256), F32),
            pltpu.VMEM((GROUP, 128, 256), F32),
        ],
        smem=1,
        args=(codes, fields, factors, press, *presses),
    )
    return density.reshape(rows), accel


def solution(mesh):
    placed = (
        P(None, ("gx", "gy")),
        P(("gx", "gy")),
        P(("gx", "gy")),
        P(("gx", "gy")),
        P(("gx", "gy"), None),
        P(None, ("gx", "gy")),
        P(("gx", "gy")),
    )
    return jax.shard_map(
        local,
        mesh=mesh,
        in_specs=placed,
        out_specs=(P(("gx", "gy")), P(None, ("gx", "gy"))),
        check_vma=False,
    )
```

```python
import functools
import math

import jax
import jax.numpy as jnp
from jax import lax
from jax.experimental import pallas as pl
from jax.experimental.pallas import tpu as pltpu
from jax.sharding import PartitionSpec as P

F32, BF16, I32 = jnp.float32, jnp.bfloat16, jnp.int32
TILE = 128
OWN = 32
GT = 8
ALL = OWN + 4 * GT
CAP = 16
BOX = 16.0
HALF = 8.0
KEYS = 48
GROUP = 8
KERNEL_NORM = 21.0 / (2.0 * math.pi)
GAMMA_LESS = 2.0 / 3.0

NT = (((1,), (1,)), ((), ()))
NN = (((1,), (0,)), ((), ()))


def iota(shape, axis):
    return lax.broadcasted_iota(I32, shape, axis)


def dot(a, b, dims=NN):
    return lax.dot_general(a, b, dims, preferred_element_type=F32)


def pieces(v):
    one = v.astype(BF16).astype(F32)
    rest = v - one
    two = rest.astype(BF16).astype(F32)
    return one, two, rest - two


def first_kernel(count, *refs):
    arguments, out, codes, held, done = refs[:6], refs[6], refs[7], refs[8:14], refs[14]
    copies = [pltpu.make_async_copy(a, b, done.at[k]) for k, (a, b) in enumerate(zip(arguments, held))]
    for copy in copies:
        copy.start()
    for copy in copies:
        copy.wait()
    dispatch(*held[:5], out)
    list_pairs(count, held[5], codes)


def dispatch(pos, mass, smooth, energy, dest, out):
    width = 256
    n = pos.shape[1]
    row = iota((width, width), 0)
    upper = (row < iota((width, width), 1)).astype(F32).astype(BF16)
    ones = jnp.ones((width, width), BF16)
    carry = jnp.zeros((width, width), F32)
    total = jnp.zeros((width, 128), F32)
    ranks = iota((CAP, width), 0)
    for b in range(n // width):
        at = slice(b * width, (b + 1) * width)
        mine = row == dest[:, at]
        hot = jnp.where(mine, 1.0, 0.0)
        hot16 = hot.astype(BF16)
        before = dot(hot16, upper) + carry
        carry = carry + dot(hot16, ones)
        rank = jnp.sum(hot * before, axis=0, keepdims=True).astype(I32)
        sel = ranks == rank
        rows = [pos[0:1, at], pos[1:2, at], pos[2:3, at], mass[:, at], smooth[:, at], energy[:, at]]
        spread = jnp.concatenate(
            [jnp.where(sel, v, 0.0) for v in rows] + [jnp.zeros((2 * CAP, width), F32)], axis=0
        )
        for piece in pieces(spread):
            total = total + dot(hot16, piece.astype(BF16), NT)
    out[...] = total


def list_pairs(count, pairs, out):
    slots = pairs.shape[1]
    target, source = pairs[0:1, :], pairs[1:2, :]
    ghost = (source >= OWN).astype(I32)
    line = jnp.where(iota((1, slots), 1) < count[0], 2 * target + ghost, -1)
    column = source - OWN * ghost
    lines = jnp.where(iota((ALL, slots), 0) == line, 1.0, 0.0).astype(BF16)
    columns = jnp.where(iota((OWN, slots), 0) == column, 1.0, 0.0).astype(BF16)
    times = dot(columns, lines, NT)
    has = jnp.where(times > 0.0, 1.0, 0.0)
    has16 = has.astype(BF16)
    lower = jnp.where(iota((OWN, OWN), 0) > iota((OWN, OWN), 1), 1.0, 0.0).astype(BF16)
    within = dot(lower, has16)
    per_line = dot(jnp.ones((OWN, OWN), BF16), has16)
    la, lb = iota((ALL, ALL), 0), iota((ALL, ALL), 1)

    ahead = jnp.where(la < lb, 1.0, 0.0).astype(BF16)
    lane = iota((OWN, ALL), 1)
    place = within + dot(per_line.astype(BF16), ahead)
    high = jnp.floor(place * (1.0 / 128.0))
    low = (place - 128.0 * high).astype(I32)
    high = jnp.where(has > 0.0, high.astype(I32), -1)
    sub = iota((OWN, ALL), 0)
    code = times * 2048.0 + ((lane // 2) * 64 + sub + (lane % 2) * OWN).astype(F32)
    total = jnp.zeros((48, 128), F32)
    parts = pieces(code)
    for k in range(OWN):
        picked = iota((16, ALL), 0) == high[k : k + 1]
        left = jnp.concatenate([jnp.where(picked, p[k : k + 1], 0.0) for p in parts], axis=0)
        right = jnp.where(iota((128, ALL), 0) == low[k : k + 1], 1.0, 0.0)
        total = total + dot(left.astype(BF16), right.astype(BF16), NT)
    out[0:16] = (total[0:16] + total[16:32] + total[32:48]).astype(I32)
    tally = jnp.sum(per_line[0:1], axis=1, keepdims=True)
    out[16:24] = jnp.broadcast_to(tally, (8, 128)).astype(I32)


def fields_of(block, shift):
    sub, lane = iota((8, 128), 0), iota((8, 128), 1) // CAP
    for bit in (1, 2, 4):
        up = pltpu.roll(pltpu.roll(block, bit, 0), 128 - CAP * bit, 1)
        down = up if bit == 4 else pltpu.roll(pltpu.roll(block, 8 - bit, 0), CAP * bit, 1)
        i, j = (sub // bit) % 2, (lane // bit) % 2
        block = jnp.where(i == j, block, jnp.where(i == 1, up, down))
    block = block - shift
    square = jnp.sum(jnp.where(sub < 3, block * block, 0.0), axis=0, keepdims=True)
    return jnp.where(sub == 6, square, jnp.where(sub == 7, 1.0, block))


def source_factor(v):
    a, b, c = pieces(v)
    return jnp.concatenate([a, a, a, b, b, c], axis=0)


def target_factor(u):
    a, b, c = pieces(u)
    return jnp.concatenate([a, b, c, a, b, a], axis=0)


def coefficients(v):
    sub = iota((8, 128), 0)
    return jnp.where(sub < 3, -2.0 * v, jnp.where(sub == 6, 1.0, jnp.where(sub == 7, v[6:7], 0.0)))


def entry(codes, e):
    code = codes[e >> 7, e & 127]
    return (code >> 6) & (OWN - 1), code & (ALL - 1), code >> 11


def sweep(codes, product, process, buffers):
    last = OWN * ALL - 1
    count = codes[16, 0]

    def load(group, buffer):
        for k in range(GROUP):
            t, s, _ = entry(codes, jnp.minimum(group * GROUP + k, last))
            buffer[k] = product(t, s)

    def work(group, buffer):
        for k in range(GROUP):
            e = group * GROUP + k
            t, s, times = entry(codes, jnp.minimum(e, last))
            process(t, s, jnp.where(e < count, times, 0), buffer, k)

    load(0, buffers[0])

    def body(i, unused):
        load(2 * i + 1, buffers[1])
        work(2 * i, buffers[0])
        load(2 * i + 2, buffers[0])
        work(2 * i + 1, buffers[1])
        return unused

    lax.fori_loop(0, (count + 2 * GROUP - 1) // (2 * GROUP), body, 0)


def density_kernel(codes, centre, moved, g0, g1, g2, g3, density, press, fields, factors, right, sums, buf0, buf1):
    sub = iota((8, 128), 0)
    shift = jnp.where(sub == 0, centre[0], jnp.where(sub == 1, centre[1], jnp.where(sub == 2, HALF, 0.0)))

    def place(tile, block):
        v = fields_of(block, shift)
        fields[tile] = v
        factors[tile] = jnp.transpose(source_factor(v)).astype(BF16)
        return v

    weigh = jnp.where(sub == 3, 4.0, 0.0)
    none = jnp.zeros((8, 128), F32)
    weigh = jnp.concatenate([weigh, none, none, weigh, none, weigh], axis=0).astype(BF16)

    def own(tile, unused):
        v = place(tile, moved[pl.ds(pl.multiple_of(tile * 8, 8), 8)])
        h = v[4:5]
        right[tile, :, 0:128] = target_factor(coefficients(v) * (1.0 / (h * h))).astype(BF16)
        right[tile, :, 128:256] = weigh
        sums[tile] = none
        return unused

    lax.fori_loop(0, OWN, own, 0, unroll=8)
    for k, ghost in enumerate((g0, g1, g2, g3)):
        there = jnp.full((8, 128), centre[2 + k], F32) > 0.0

        def other(tile, unused):
            block = ghost[pl.ds(pl.multiple_of(tile * 8, 8), 8)]
            place(OWN + k * GT + tile, jnp.where(there, block, 0.0))
            return unused

        lax.fori_loop(0, GT, other, 0, unroll=8)

    def product(t, s):
        return dot(factors[s], right[t])

    def process(t, s, times, buffer, k):
        ratio_sq = jnp.maximum(buffer[k, :, 0:128], 1e-30)
        ratio = ratio_sq * lax.rsqrt(ratio_sq)
        falloff = jnp.maximum(1.0 - ratio, 0.0)
        falloff = falloff * falloff
        falloff = falloff * falloff
        term = falloff * (ratio + 0.25) * buffer[k, :, 128:256]
        sums[t] += jnp.sum(term.reshape(16, 8, 128), axis=0) * jnp.full((8, 128), times, I32).astype(F32)

    sweep(codes, product, process, (buf0, buf1))
    total = jnp.sum(sums[...], axis=1)
    h = fields[0:OWN, 4, :]
    result = KERNEL_NORM / (h * h * h) * (total + fields[0:OWN, 3, :])
    density[...] = result
    press[...] = GAMMA_LESS * fields[0:OWN, 5, :] / result


def accel_kernel(codes, fields, factors, press, p0, p1, p2, p3, accel, right, pulls, sums, buf0, buf1):
    sub = iota((8, 128), 0)
    none = jnp.zeros((8, 128), F32)

    def pull(tile, p):
        v = fields[tile]
        x = jnp.where(sub < 4, pltpu.roll(v, 1, 0), pltpu.roll(v, 5, 0))
        x = jnp.where(sub % 4 == 0, 1.0, x) * v[3:4]
        x = jnp.where(sub < 4, x, x * p)
        both = jnp.concatenate([*pieces(x), none], axis=0).astype(BF16)
        pulls[tile, :, 0:128] = both
        pulls[tile, :, 128:256] = both
        return v

    def own(tile, unused):
        v = pull(tile, press[pl.ds(tile, 1)])
        right[tile, :, 0:128] = target_factor(coefficients(v)).astype(BF16)
        h = jnp.where(sub == 4, 1.0, jnp.where(sub == 7, v[4:5], 0.0))
        right[tile, :, 128:256] = target_factor(h).astype(BF16)
        sums[tile] = jnp.zeros((32, 128), F32)
        return unused

    lax.fori_loop(0, OWN, own, 0, unroll=8)
    for k, ghost in enumerate((p0, p1, p2, p3)):

        def other(tile, unused):
            pull(OWN + k * GT + tile, ghost[pl.ds(tile, 1)])
            return unused

        lax.fori_loop(0, GT, other, 0, unroll=8)

    def product(t, s):
        return dot(factors[s], right[t])

    def process(t, s, times, buffer, k):
        dist_sq = jnp.maximum(buffer[k, :, 0:128], 1e-30)
        near = 1.0 / buffer[k, :, 128:256]
        near_sq = near * near
        gap = jnp.maximum(near - dist_sq * lax.rsqrt(dist_sq) * (2.0 * near_sq), 0.0)
        slope = gap * gap * gap * near_sq
        first = slope.astype(BF16)
        second = (slope - first.astype(F32)).astype(BF16)
        both = jnp.concatenate([first, second], axis=0)
        sums[t] += dot(pulls[s], both) * jnp.full((32, 128), times, I32).astype(F32)

    sweep(codes, product, process, (buf0, buf1))

    def finish(tile, unused):
        v = fields[tile]
        s = sums[tile]
        s = s[0:8] + s[8:16] + s[16:24]
        p = press[pl.ds(tile, 1)]
        a = p * (v * s[0:1] - pltpu.roll(s, 7, 0)) + (v * s[4:5] - pltpu.roll(s, 3, 0))
        accel[:, pl.ds(pl.multiple_of(tile * 128, 128), 128)] = a[0:3] * (640.0 * KERNEL_NORM)
        return unused

    lax.fori_loop(0, OWN, finish, 0)


def call(kernel, shapes, scratch=(), smem=0, args=(), space=pltpu.VMEM, limit=40):
    specs = [pl.BlockSpec(memory_space=pltpu.SMEM)] * smem
    specs += [pl.BlockSpec(memory_space=space)] * (len(args) - smem)
    return pl.pallas_call(
        kernel,
        out_shape=[jax.ShapeDtypeStruct(s, d) for s, d in shapes],
        in_specs=specs,
        out_specs=[pl.BlockSpec(memory_space=pltpu.VMEM)] * len(shapes),
        scratch_shapes=list(scratch),
        compiler_params=pltpu.CompilerParams(vmem_limit_bytes=limit * 2**20),
    )(*args)


def around(edge):
    taken = []
    for axis in ("gx", "gy"):
        count = lax.axis_size(axis)
        forward = [(i, (i + 1) % count) for i in range(count)]
        taken.append(lax.ppermute(edge, axis, forward))
        taken.append(lax.ppermute(edge, axis, [(b, a) for a, b in forward]))
    return taken


def local(positions, mass, smoothing, energy, destination, pairs, pair_count):
    rows = mass.shape[0]
    flat = [a.reshape(1, rows) for a in (mass, smoothing, energy, destination)]
    given = (positions, *flat, pairs)
    outgoing, codes = call(
        first_kernel,
        [((256, 128), F32), ((24, 128), I32)],
        scratch=[pltpu.VMEM(a.shape, a.dtype) for a in given] + [pltpu.SemaphoreType.DMA((len(given),))],
        smem=1,
        args=(pair_count, *given),
        space=pl.ANY,
        limit=60,
    )
    moved = lax.all_to_all(outgoing, ("gx", "gy"), split_axis=0, concat_axis=0, tiled=True)
    ghosts = around(moved[: GT * 8])
    i, j = lax.axis_index("gx"), lax.axis_index("gy")
    there = [i > 0, i < lax.axis_size("gx") - 1, j > 0, j < lax.axis_size("gy") - 1]
    centre = jnp.stack([i.astype(F32) * BOX + HALF, j.astype(F32) * BOX + HALF] + [t.astype(F32) for t in there])
    density, press, fields, factors = call(
        density_kernel,
        [((OWN, 128), F32), ((OWN, 128), F32), ((ALL, 8, 128), F32), ((ALL, 128, KEYS), BF16)],
        scratch=[
            pltpu.VMEM((OWN, KEYS, 256), BF16),
            pltpu.VMEM((OWN, 8, 128), F32),
            pltpu.VMEM((GROUP, 128, 256), F32),
            pltpu.VMEM((GROUP, 128, 256), F32),
        ],
        smem=2,
        args=(codes, centre, moved, *ghosts),
    )
    presses = around(press[:GT])
    (accel,) = call(
        accel_kernel,
        [((3, rows), F32)],
        scratch=[
            pltpu.VMEM((OWN, KEYS, 256), BF16),
            pltpu.VMEM((ALL, 32, 256), BF16),
            pltpu.VMEM((OWN, 32, 128), F32),
            pltpu.VMEM((GROUP, 128, 256), F32),
            pltpu.VMEM((GROUP, 128, 256), F32),
        ],
        smem=1,
        args=(codes, fields, factors, press, *presses),
    )
    return density.reshape(rows), accel


def solution(mesh):
    placed = (
        P(None, ("gx", "gy")),
        P(("gx", "gy")),
        P(("gx", "gy")),
        P(("gx", "gy")),
        P(("gx", "gy"), None),
        P(None, ("gx", "gy")),
        P(("gx", "gy")),
    )
    return jax.shard_map(
        local,
        mesh=mesh,
        in_specs=placed,
        out_specs=(P(("gx", "gy")), P(None, ("gx", "gy"))),
        check_vma=False,
    )
```

```python
import functools
import math

import jax
import jax.numpy as jnp
from jax import lax
from jax.experimental import pallas as pl
from jax.experimental.pallas import tpu as pltpu
from jax.sharding import PartitionSpec as P

F32, BF16, I32 = jnp.float32, jnp.bfloat16, jnp.int32
TILE = 128
OWN = 32
GT = 8
ALL = OWN + 4 * GT
CAP = 16
BOX = 16.0
HALF = 8.0
KEYS = 48
DEPTH = (24, 20)
KERNEL_NORM = 21.0 / (2.0 * math.pi)
GAMMA_LESS = 2.0 / 3.0

NT = (((1,), (1,)), ((), ()))
NN = (((1,), (0,)), ((), ()))


def iota(shape, axis):
    return lax.broadcasted_iota(I32, shape, axis)


def dot(a, b, dims=NN):
    return lax.dot_general(a, b, dims, preferred_element_type=F32)


def pieces(v):
    one = v.astype(BF16).astype(F32)
    rest = v - one
    two = rest.astype(BF16).astype(F32)
    return one, two, rest - two


def first_kernel(count, *refs):
    arguments, out, codes, held, done = refs[:6], refs[6], refs[7], refs[8:14], refs[14]
    copies = [pltpu.make_async_copy(a, b, done.at[k]) for k, (a, b) in enumerate(zip(arguments, held))]
    for copy in copies:
        copy.start()
    for copy in copies:
        copy.wait()
    dispatch(*held[:5], out)
    list_pairs(count, held[5], codes)


def dispatch(pos, mass, smooth, energy, dest, out):
    width = 256
    n = pos.shape[1]
    row = iota((width, width), 0)
    upper = (row < iota((width, width), 1)).astype(F32).astype(BF16)
    ones = jnp.ones((width, width), BF16)
    carry = jnp.zeros((width, width), F32)
    total = jnp.zeros((width, 128), F32)
    ranks = iota((CAP, width), 0)
    for b in range(n // width):
        at = slice(b * width, (b + 1) * width)
        mine = row == dest[:, at]
        hot = jnp.where(mine, 1.0, 0.0)
        hot16 = hot.astype(BF16)
        before = dot(hot16, upper) + carry
        carry = carry + dot(hot16, ones)
        rank = jnp.sum(hot * before, axis=0, keepdims=True).astype(I32)
        sel = ranks == rank
        rows = [pos[0:1, at], pos[1:2, at], pos[2:3, at], mass[:, at], smooth[:, at], energy[:, at]]
        spread = jnp.concatenate(
            [jnp.where(sel, v, 0.0) for v in rows] + [jnp.zeros((2 * CAP, width), F32)], axis=0
        )
        for piece in pieces(spread):
            total = total + dot(hot16, piece.astype(BF16), NT)
    out[...] = total


def list_pairs(count, pairs, out):
    slots = pairs.shape[1]
    target, source = pairs[0:1, :], pairs[1:2, :]
    ghost = (source >= OWN).astype(I32)
    line = jnp.where(iota((1, slots), 1) < count[0], 2 * target + ghost, -1)
    column = source - OWN * ghost
    lines = jnp.where(iota((ALL, slots), 0) == line, 1.0, 0.0).astype(BF16)
    columns = jnp.where(iota((OWN, slots), 0) == column, 1.0, 0.0).astype(BF16)
    times = dot(columns, lines, NT)
    has = jnp.where(times > 0.0, 1.0, 0.0)
    has16 = has.astype(BF16)
    lower = jnp.where(iota((OWN, OWN), 0) > iota((OWN, OWN), 1), 1.0, 0.0).astype(BF16)
    within = dot(lower, has16)
    per_line = dot(jnp.ones((OWN, OWN), BF16), has16)
    la, lb = iota((ALL, ALL), 0), iota((ALL, ALL), 1)

    ahead = jnp.where(la < lb, 1.0, 0.0).astype(BF16)
    lane = iota((OWN, ALL), 1)
    place = within + dot(per_line.astype(BF16), ahead)
    high = jnp.floor(place * (1.0 / 128.0))
    low = (place - 128.0 * high).astype(I32)
    high = jnp.where(has > 0.0, high.astype(I32), -1)
    sub = iota((OWN, ALL), 0)
    code = times * 2048.0 + ((lane // 2) * 64 + sub + (lane % 2) * OWN).astype(F32)
    total = jnp.zeros((48, 128), F32)
    parts = pieces(code)
    for k in range(OWN):
        picked = iota((16, ALL), 0) == high[k : k + 1]
        left = jnp.concatenate([jnp.where(picked, p[k : k + 1], 0.0) for p in parts], axis=0)
        right = jnp.where(iota((128, ALL), 0) == low[k : k + 1], 1.0, 0.0)
        total = total + dot(left.astype(BF16), right.astype(BF16), NT)
    out[0:16] = (total[0:16] + total[16:32] + total[32:48]).astype(I32)
    tally = jnp.sum(per_line[0:1], axis=1, keepdims=True)
    out[16:24] = jnp.broadcast_to(tally, (8, 128)).astype(I32)


def fields_of(block, shift):
    sub, lane = iota((8, 128), 0), iota((8, 128), 1) // CAP
    for bit in (1, 2, 4):
        up = pltpu.roll(pltpu.roll(block, bit, 0), 128 - CAP * bit, 1)
        down = up if bit == 4 else pltpu.roll(pltpu.roll(block, 8 - bit, 0), CAP * bit, 1)
        i, j = (sub // bit) % 2, (lane // bit) % 2
        block = jnp.where(i == j, block, jnp.where(i == 1, up, down))
    block = block - shift
    square = jnp.sum(jnp.where(sub < 3, block * block, 0.0), axis=0, keepdims=True)
    return jnp.where(sub == 6, square, jnp.where(sub == 7, 1.0, block))


def source_factor(v):
    a, b, c = pieces(v)
    return jnp.concatenate([a, a, a, b, b, c], axis=0)


def target_factor(u):
    a, b, c = pieces(u)
    return jnp.concatenate([a, b, c, a, b, a], axis=0)


def coefficients(v):
    sub = iota((8, 128), 0)
    return jnp.where(sub < 3, -2.0 * v, jnp.where(sub == 6, 1.0, jnp.where(sub == 7, v[6:7], 0.0)))


def entry(codes, e):
    code = codes[e >> 7, e & 127]
    return (code >> 6) & (OWN - 1), code & (ALL - 1), code >> 11


def sweep(codes, product, process, buffers):
    turns, depth = len(buffers), buffers[0].shape[0]
    last = OWN * ALL - 1
    count = codes[16, 0]

    def load(e, buffer, k):
        t, s, _ = entry(codes, jnp.minimum(e, last))
        buffer[k] = product(t, s)

    def work(e, buffer, k):
        t, s, times = entry(codes, jnp.minimum(e, last))
        process(t, s, jnp.where(e < count, times, 0), buffer, k)

    for k in range(depth):
        load(k, buffers[0], k)

    def body(i, unused):
        for turn in range(turns):
            for k in range(depth):
                e = (i * turns + turn) * depth + k
                if turns == 1:
                    work(e, buffers[0], k)
                    load(e + depth, buffers[0], k)
                else:
                    load(e + depth, buffers[1 - turn], k)
                    work(e, buffers[turn], k)
        return unused

    lax.fori_loop(0, (count + turns * depth - 1) // (turns * depth), body, 0)


def density_kernel(codes, centre, moved, g0, g1, g2, g3, density, press, fields, factors, right, sums, buffer):
    sub = iota((8, 128), 0)
    shift = jnp.where(sub == 0, centre[0], jnp.where(sub == 1, centre[1], jnp.where(sub == 2, HALF, 0.0)))

    def place(tile, block):
        v = fields_of(block, shift)
        fields[tile] = v
        factors[tile] = jnp.transpose(source_factor(v)).astype(BF16)
        return v

    weigh = jnp.where(sub == 3, 4.0, 0.0)
    none = jnp.zeros((8, 128), F32)
    weigh = jnp.concatenate([weigh, none, none, weigh, none, weigh], axis=0).astype(BF16)

    def own(tile, unused):
        v = place(tile, moved[pl.ds(pl.multiple_of(tile * 8, 8), 8)])
        h = v[4:5]
        right[tile, :, 0:128] = target_factor(coefficients(v) * (1.0 / (h * h))).astype(BF16)
        right[tile, :, 128:256] = weigh
        sums[tile] = none
        return unused

    lax.fori_loop(0, OWN, own, 0, unroll=8)
    for k, ghost in enumerate((g0, g1, g2, g3)):
        there = jnp.full((8, 128), centre[2 + k], F32) > 0.0

        def other(tile, unused):
            block = ghost[pl.ds(pl.multiple_of(tile * 8, 8), 8)]
            place(OWN + k * GT + tile, jnp.where(there, block, 0.0))
            return unused

        lax.fori_loop(0, GT, other, 0, unroll=8)

    def product(t, s):
        return dot(factors[s], right[t])

    def process(t, s, times, buffer, k):
        ratio_sq = jnp.maximum(buffer[k, :, 0:128], 1e-30)
        ratio = ratio_sq * lax.rsqrt(ratio_sq)
        falloff = jnp.maximum(1.0 - ratio, 0.0)
        falloff = falloff * falloff
        falloff = falloff * falloff
        term = falloff * (ratio + 0.25) * buffer[k, :, 128:256]
        sums[t] += jnp.sum(term.reshape(16, 8, 128), axis=0) * jnp.full((8, 128), times, I32).astype(F32)

    sweep(codes, product, process, (buffer,))
    total = jnp.sum(sums[...], axis=1)
    h = fields[0:OWN, 4, :]
    result = KERNEL_NORM / (h * h * h) * (total + fields[0:OWN, 3, :])
    density[...] = result
    press[...] = GAMMA_LESS * fields[0:OWN, 5, :] / result


def accel_kernel(codes, fields, factors, press, p0, p1, p2, p3, accel, right, pulls, sums, buf0, buf1):
    sub = iota((8, 128), 0)
    none = jnp.zeros((8, 128), F32)

    def pull(tile, p):
        v = fields[tile]
        x = jnp.where(sub < 4, pltpu.roll(v, 1, 0), pltpu.roll(v, 5, 0))
        x = jnp.where(sub % 4 == 0, 1.0, x) * v[3:4]
        x = jnp.where(sub < 4, x, x * p)
        both = jnp.concatenate([*pieces(x), none], axis=0).astype(BF16)
        pulls[tile, :, 0:128] = both
        pulls[tile, :, 128:256] = both
        return v

    def own(tile, unused):
        v = pull(tile, press[pl.ds(tile, 1)])
        right[tile, :, 0:128] = target_factor(4.0 * coefficients(v)).astype(BF16)
        h = jnp.where(sub == 4, 1.0, jnp.where(sub == 7, v[4:5], 0.0))
        right[tile, :, 128:256] = target_factor(h).astype(BF16)
        sums[tile] = jnp.zeros((32, 128), F32)
        return unused

    lax.fori_loop(0, OWN, own, 0, unroll=8)
    for k, ghost in enumerate((p0, p1, p2, p3)):

        def other(tile, unused):
            pull(OWN + k * GT + tile, ghost[pl.ds(tile, 1)])
            return unused

        lax.fori_loop(0, GT, other, 0, unroll=8)

    def product(t, s):
        return dot(factors[s], right[t])

    def process(t, s, times, buffer, k):
        dist_sq = jnp.maximum(buffer[k, :, 0:128], 1e-30)
        near = 1.0 / buffer[k, :, 128:256]
        near_sq = near * near
        gap = jnp.maximum(near - dist_sq * lax.rsqrt(dist_sq) * near_sq, 0.0)
        slope = gap * gap * gap * near_sq
        first = slope.astype(BF16)
        second = (slope - first.astype(F32)).astype(BF16)
        both = jnp.concatenate([first, second], axis=0)
        sums[t] += dot(pulls[s], both) * jnp.full((32, 128), times, I32).astype(F32)

    sweep(codes, product, process, (buf0, buf1))

    def finish(tile, unused):
        v = fields[tile]
        s = sums[tile]
        s = s[0:8] + s[8:16] + s[16:24]
        p = press[pl.ds(tile, 1)]
        a = p * (v * s[0:1] - pltpu.roll(s, 7, 0)) + (v * s[4:5] - pltpu.roll(s, 3, 0))
        accel[:, pl.ds(pl.multiple_of(tile * 128, 128), 128)] = a[0:3] * (640.0 * KERNEL_NORM)
        return unused

    lax.fori_loop(0, OWN, finish, 0)


def call(kernel, shapes, scratch=(), smem=0, args=(), space=pltpu.VMEM, limit=40):
    specs = [pl.BlockSpec(memory_space=pltpu.SMEM)] * smem
    specs += [pl.BlockSpec(memory_space=space)] * (len(args) - smem)
    return pl.pallas_call(
        kernel,
        out_shape=[jax.ShapeDtypeStruct(s, d) for s, d in shapes],
        in_specs=specs,
        out_specs=[pl.BlockSpec(memory_space=pltpu.VMEM)] * len(shapes),
        scratch_shapes=list(scratch),
        compiler_params=pltpu.CompilerParams(vmem_limit_bytes=limit * 2**20),
    )(*args)


def around(edge):
    taken = []
    for axis in ("gx", "gy"):
        count = lax.axis_size(axis)
        forward = [(i, (i + 1) % count) for i in range(count)]
        taken.append(lax.ppermute(edge, axis, forward))
        taken.append(lax.ppermute(edge, axis, [(b, a) for a, b in forward]))
    return taken


def local(positions, mass, smoothing, energy, destination, pairs, pair_count):
    rows = mass.shape[0]
    flat = [a.reshape(1, rows) for a in (mass, smoothing, energy, destination)]
    given = (positions, *flat, pairs)
    outgoing, codes = call(
        first_kernel,
        [((256, 128), F32), ((24, 128), I32)],
        scratch=[pltpu.VMEM(a.shape, a.dtype) for a in given] + [pltpu.SemaphoreType.DMA((len(given),))],
        smem=1,
        args=(pair_count, *given),
        space=pl.ANY,
        limit=60,
    )
    moved = lax.all_to_all(outgoing, ("gx", "gy"), split_axis=0, concat_axis=0, tiled=True)
    ghosts = around(moved[: GT * 8])
    i, j = lax.axis_index("gx"), lax.axis_index("gy")
    there = [i > 0, i < lax.axis_size("gx") - 1, j > 0, j < lax.axis_size("gy") - 1]
    centre = jnp.stack([i.astype(F32) * BOX + HALF, j.astype(F32) * BOX + HALF] + [t.astype(F32) for t in there])
    density, press, fields, factors = call(
        density_kernel,
        [((OWN, 128), F32), ((OWN, 128), F32), ((ALL, 8, 128), F32), ((ALL, 128, KEYS), BF16)],
        scratch=[
            pltpu.VMEM((OWN, KEYS, 256), BF16),
            pltpu.VMEM((OWN, 8, 128), F32),
            pltpu.VMEM((DEPTH[0], 128, 256), F32),
        ],
        smem=2,
        args=(codes, centre, moved, *ghosts),
    )
    presses = around(press[:GT])
    (accel,) = call(
        accel_kernel,
        [((3, rows), F32)],
        scratch=[
            pltpu.VMEM((OWN, KEYS, 256), BF16),
            pltpu.VMEM((ALL, 32, 256), BF16),
            pltpu.VMEM((OWN, 32, 128), F32),
            pltpu.VMEM((DEPTH[1], 128, 256), F32),
            pltpu.VMEM((DEPTH[1], 128, 256), F32),
        ],
        smem=1,
        args=(codes, fields, factors, press, *presses),
    )
    return density.reshape(rows), accel


def solution(mesh):
    placed = (
        P(None, ("gx", "gy")),
        P(("gx", "gy")),
        P(("gx", "gy")),
        P(("gx", "gy")),
        P(("gx", "gy"), None),
        P(None, ("gx", "gy")),
        P(("gx", "gy")),
    )
    return jax.shard_map(
        local,
        mesh=mesh,
        in_specs=placed,
        out_specs=(P(("gx", "gy")), P(None, ("gx", "gy"))),
        check_vma=False,
    )
```

```python
import functools
import math

import jax
import jax.numpy as jnp
from jax import lax
from jax.experimental import pallas as pl
from jax.experimental.pallas import tpu as pltpu
from jax.sharding import PartitionSpec as P

F32, BF16, I32 = jnp.float32, jnp.bfloat16, jnp.int32
TILE = 128
OWN = 32
GT = 8
ALL = OWN + 4 * GT
CAP = 16
BOX = 16.0
HALF = 8.0
KEYS = 48
DEPTH = (24, 20)
KERNEL_NORM = 21.0 / (2.0 * math.pi)
GAMMA_LESS = 2.0 / 3.0

NT = (((1,), (1,)), ((), ()))
NN = (((1,), (0,)), ((), ()))


def iota(shape, axis):
    return lax.broadcasted_iota(I32, shape, axis)


def dot(a, b, dims=NN):
    return lax.dot_general(a, b, dims, preferred_element_type=F32)


def pieces(v):
    one = v.astype(BF16).astype(F32)
    rest = v - one
    two = rest.astype(BF16).astype(F32)
    return one, two, rest - two


def first_kernel(*refs):
    arguments, out, held, done = refs[:6], refs[6], refs[8:13] + (refs[7],), refs[13]
    copies = [pltpu.make_async_copy(a, b, done.at[k]) for k, (a, b) in enumerate(zip(arguments, held))]
    for copy in copies:
        copy.start()
    for copy in copies:
        copy.wait()
    dispatch(*held[:5], out)


def dispatch(pos, mass, smooth, energy, dest, out):
    width = 256
    n = pos.shape[1]
    row = iota((width, width), 0)
    upper = (row < iota((width, width), 1)).astype(F32).astype(BF16)
    ones = jnp.ones((width, width), BF16)
    carry = jnp.zeros((width, width), F32)
    total = jnp.zeros((width, 128), F32)
    ranks = iota((CAP, width), 0)
    for b in range(n // width):
        at = slice(b * width, (b + 1) * width)
        mine = row == dest[:, at]
        hot = jnp.where(mine, 1.0, 0.0)
        hot16 = hot.astype(BF16)
        before = dot(hot16, upper) + carry
        carry = carry + dot(hot16, ones)
        rank = jnp.sum(hot * before, axis=0, keepdims=True).astype(I32)
        sel = ranks == rank
        rows = [pos[0:1, at], pos[1:2, at], pos[2:3, at], mass[:, at], smooth[:, at], energy[:, at]]
        spread = jnp.concatenate(
            [jnp.where(sel, v, 0.0) for v in rows] + [jnp.zeros((2 * CAP, width), F32)], axis=0
        )
        for piece in pieces(spread):
            total = total + dot(hot16, piece.astype(BF16), NT)
    out[...] = total


def list_pairs(count, pairs, out):
    slots = pairs.shape[1]
    target, source = pairs[0:1, :], pairs[1:2, :]
    ghost = (source >= OWN).astype(I32)
    line = jnp.where(iota((1, slots), 1) < count[0], 2 * target + ghost, -1)
    column = source - OWN * ghost
    lines = jnp.where(iota((ALL, slots), 0) == line, 1.0, 0.0).astype(BF16)
    columns = jnp.where(iota((OWN, slots), 0) == column, 1.0, 0.0).astype(BF16)
    times = dot(columns, lines, NT)
    has = jnp.where(times > 0.0, 1.0, 0.0)
    has16 = has.astype(BF16)
    lower = jnp.where(iota((OWN, OWN), 0) > iota((OWN, OWN), 1), 1.0, 0.0).astype(BF16)
    within = dot(lower, has16)
    per_line = dot(jnp.ones((OWN, OWN), BF16), has16)
    la, lb = iota((ALL, ALL), 0), iota((ALL, ALL), 1)

    ahead = jnp.where(la < lb, 1.0, 0.0).astype(BF16)
    lane = iota((OWN, ALL), 1)
    place = within + dot(per_line.astype(BF16), ahead)
    high = jnp.floor(place * (1.0 / 128.0))
    low = (place - 128.0 * high).astype(I32)
    high = jnp.where(has > 0.0, high.astype(I32), -1)
    sub = iota((OWN, ALL), 0)
    code = times * 2048.0 + ((lane // 2) * 64 + sub + (lane % 2) * OWN).astype(F32)
    total = jnp.zeros((48, 128), F32)
    parts = pieces(code)
    for k in range(OWN):
        picked = iota((16, ALL), 0) == high[k : k + 1]
        left = jnp.concatenate([jnp.where(picked, p[k : k + 1], 0.0) for p in parts], axis=0)
        right = jnp.where(iota((128, ALL), 0) == low[k : k + 1], 1.0, 0.0)
        total = total + dot(left.astype(BF16), right.astype(BF16), NT)
    out[0:16] = (total[0:16] + total[16:32] + total[32:48]).astype(I32)
    tally = jnp.sum(per_line[0:1], axis=1, keepdims=True)
    out[16:24] = jnp.broadcast_to(tally, (8, 128)).astype(I32)


def fields_of(block, shift):
    sub, lane = iota((8, 128), 0), iota((8, 128), 1) // CAP
    for bit in (1, 2, 4):
        up = pltpu.roll(pltpu.roll(block, bit, 0), 128 - CAP * bit, 1)
        down = up if bit == 4 else pltpu.roll(pltpu.roll(block, 8 - bit, 0), CAP * bit, 1)
        i, j = (sub // bit) % 2, (lane // bit) % 2
        block = jnp.where(i == j, block, jnp.where(i == 1, up, down))
    block = block - shift
    square = jnp.sum(jnp.where(sub < 3, block * block, 0.0), axis=0, keepdims=True)
    return jnp.where(sub == 6, square, jnp.where(sub == 7, 1.0, block))


def source_factor(v):
    a, b, c = pieces(v)
    return jnp.concatenate([a, a, a, b, b, c], axis=0)


def target_factor(u):
    a, b, c = pieces(u)
    return jnp.concatenate([a, b, c, a, b, a], axis=0)


def coefficients(v):
    sub = iota((8, 128), 0)
    return jnp.where(sub < 3, -2.0 * v, jnp.where(sub == 6, 1.0, jnp.where(sub == 7, v[6:7], 0.0)))


def entry(codes, e):
    code = codes[e >> 7, e & 127]
    return (code >> 6) & (OWN - 1), code & (ALL - 1), code >> 11


def sweep(codes, product, process, buffers):
    turns, depth = len(buffers), buffers[0].shape[0]
    last = OWN * ALL - 1
    count = codes[16, 0]

    def load(e, buffer, k):
        t, s, _ = entry(codes, jnp.minimum(e, last))
        buffer[k] = product(t, s)

    def work(e, buffer, k):
        t, s, times = entry(codes, jnp.minimum(e, last))
        process(t, s, jnp.where(e < count, times, 0), buffer, k)

    for k in range(depth):
        load(k, buffers[0], k)

    def body(i, unused):
        for turn in range(turns):
            for k in range(depth):
                e = (i * turns + turn) * depth + k
                if turns == 1:
                    work(e, buffers[0], k)
                    load(e + depth, buffers[0], k)
                else:
                    load(e + depth, buffers[1 - turn], k)
                    work(e, buffers[turn], k)
        return unused

    lax.fori_loop(0, (count + turns * depth - 1) // (turns * depth), body, 0)


def origin(centre):
    sub = iota((8, 128), 0)
    return jnp.where(sub == 0, centre[0], jnp.where(sub == 1, centre[1], jnp.where(sub == 2, HALF, 0.0)))


def place(tile, block, shift, fields, factors):
    v = fields_of(block, shift)
    fields[tile] = v
    factors[tile] = jnp.transpose(source_factor(v)).astype(BF16)
    return v


def prepare_kernel(count, centre, pairs, moved, codes, fields, factors, right):
    shift = origin(centre)
    none = jnp.zeros((8, 128), F32)
    weigh = jnp.where(iota((8, 128), 0) == 3, 4.0, 0.0)
    weigh = jnp.concatenate([weigh, none, none, weigh, none, weigh], axis=0).astype(BF16)
    list_pairs(count, pairs, codes)

    def own(tile, unused):
        v = place(tile, moved[pl.ds(pl.multiple_of(tile * 8, 8), 8)], shift, fields, factors)
        h = v[4:5]
        right[tile, :, 0:128] = target_factor(coefficients(v) * (1.0 / (h * h))).astype(BF16)
        right[tile, :, 128:256] = weigh
        return unused

    lax.fori_loop(0, OWN, own, 0, unroll=8)


def density_kernel(codes, centre, own_fields, own_factors, right, g0, g1, g2, g3, density, press, fields, factors, sums, buffer):
    shift = origin(centre)
    fields[0:OWN] = own_fields[...]
    factors[0:OWN] = own_factors[...]
    sums[...] = jnp.zeros((OWN, 8, 128), F32)
    for k, ghost in enumerate((g0, g1, g2, g3)):
        there = jnp.full((8, 128), centre[2 + k], F32) > 0.0

        def other(tile, unused):
            block = ghost[pl.ds(pl.multiple_of(tile * 8, 8), 8)]
            place(OWN + k * GT + tile, jnp.where(there, block, 0.0), shift, fields, factors)
            return unused

        lax.fori_loop(0, GT, other, 0, unroll=8)

    def product(t, s):
        return dot(factors[s], right[t])

    def process(t, s, times, buffer, k):
        ratio_sq = jnp.maximum(buffer[k, :, 0:128], 1e-30)
        ratio = ratio_sq * lax.rsqrt(ratio_sq)
        falloff = jnp.maximum(1.0 - ratio, 0.0)
        falloff = falloff * falloff
        falloff = falloff * falloff
        term = falloff * (ratio + 0.25) * buffer[k, :, 128:256]
        sums[t] += jnp.sum(term.reshape(16, 8, 128), axis=0) * jnp.full((8, 128), times, I32).astype(F32)

    sweep(codes, product, process, (buffer,))
    total = jnp.sum(sums[...], axis=1)
    h = fields[0:OWN, 4, :]
    result = KERNEL_NORM / (h * h * h) * (total + fields[0:OWN, 3, :])
    density[...] = result
    press[...] = GAMMA_LESS * fields[0:OWN, 5, :] / result


def pull(tile, v, p, pulls):
    sub = iota((8, 128), 0)
    x = jnp.where(sub < 4, pltpu.roll(v, 1, 0), pltpu.roll(v, 5, 0))
    x = jnp.where(sub % 4 == 0, 1.0, x) * v[3:4]
    x = jnp.where(sub < 4, x, x * p)
    both = jnp.concatenate([*pieces(x), jnp.zeros((8, 128), F32)], axis=0).astype(BF16)
    pulls[tile, :, 0:128] = both
    pulls[tile, :, 128:256] = both


def between_kernel(fields, press, pulls, right):
    sub = iota((8, 128), 0)

    def own(tile, unused):
        v = fields[tile]
        pull(tile, v, press[pl.ds(tile, 1)], pulls)
        right[tile, :, 0:128] = target_factor(4.0 * coefficients(v)).astype(BF16)
        h = jnp.where(sub == 4, 1.0, jnp.where(sub == 7, v[4:5], 0.0))
        right[tile, :, 128:256] = target_factor(h).astype(BF16)
        return unused

    lax.fori_loop(0, OWN, own, 0, unroll=8)


def accel_kernel(codes, fields, factors, own_pulls, right, press, p0, p1, p2, p3, accel, pulls, sums, buf0, buf1):
    pulls[0:OWN] = own_pulls[...]
    sums[...] = jnp.zeros((OWN, 32, 128), F32)
    for k, ghost in enumerate((p0, p1, p2, p3)):

        def other(tile, unused):
            pull(OWN + k * GT + tile, fields[OWN + k * GT + tile], ghost[pl.ds(tile, 1)], pulls)
            return unused

        lax.fori_loop(0, GT, other, 0, unroll=8)

    def product(t, s):
        return dot(factors[s], right[t])

    def process(t, s, times, buffer, k):
        dist_sq = jnp.maximum(buffer[k, :, 0:128], 1e-30)
        near = 1.0 / buffer[k, :, 128:256]
        near_sq = near * near
        gap = jnp.maximum(near - dist_sq * lax.rsqrt(dist_sq) * near_sq, 0.0)
        slope = gap * gap * gap * near_sq
        first = slope.astype(BF16)
        second = (slope - first.astype(F32)).astype(BF16)
        both = jnp.concatenate([first, second], axis=0)
        sums[t] += dot(pulls[s], both) * jnp.full((32, 128), times, I32).astype(F32)

    sweep(codes, product, process, (buf0, buf1))

    def finish(tile, unused):
        v = fields[tile]
        s = sums[tile]
        s = s[0:8] + s[8:16] + s[16:24]
        p = press[pl.ds(tile, 1)]
        a = p * (v * s[0:1] - pltpu.roll(s, 7, 0)) + (v * s[4:5] - pltpu.roll(s, 3, 0))
        accel[:, pl.ds(pl.multiple_of(tile * 128, 128), 128)] = a[0:3] * (640.0 * KERNEL_NORM)
        return unused

    lax.fori_loop(0, OWN, finish, 0)


def call(kernel, shapes, scratch=(), smem=0, args=(), space=pltpu.VMEM, limit=40):
    specs = [pl.BlockSpec(memory_space=pltpu.SMEM)] * smem
    specs += [pl.BlockSpec(memory_space=space)] * (len(args) - smem)
    return pl.pallas_call(
        kernel,
        out_shape=[jax.ShapeDtypeStruct(s, d) for s, d in shapes],
        in_specs=specs,
        out_specs=[pl.BlockSpec(memory_space=pltpu.VMEM)] * len(shapes),
        scratch_shapes=list(scratch),
        compiler_params=pltpu.CompilerParams(vmem_limit_bytes=limit * 2**20),
    )(*args)


def around(edge):
    taken = []
    for axis in ("gx", "gy"):
        count = lax.axis_size(axis)
        forward = [(i, (i + 1) % count) for i in range(count)]
        taken.append(lax.ppermute(edge, axis, forward))
        taken.append(lax.ppermute(edge, axis, [(b, a) for a, b in forward]))
    return taken


def local(positions, mass, smoothing, energy, destination, pairs, pair_count):
    rows = mass.shape[0]
    flat = [a.reshape(1, rows) for a in (mass, smoothing, energy, destination)]
    given = (positions, *flat, pairs)
    outgoing, listed = call(
        first_kernel,
        [((256, 128), F32), (pairs.shape, I32)],
        scratch=[pltpu.VMEM(a.shape, a.dtype) for a in given[:5]] + [pltpu.SemaphoreType.DMA((len(given),))],
        args=given,
        space=pl.ANY,
        limit=60,
    )
    moved = lax.all_to_all(outgoing, ("gx", "gy"), split_axis=0, concat_axis=0, tiled=True)
    ghosts = around(moved[: GT * 8])
    i, j = lax.axis_index("gx"), lax.axis_index("gy")
    there = [i > 0, i < lax.axis_size("gx") - 1, j > 0, j < lax.axis_size("gy") - 1]
    centre = jnp.stack([i.astype(F32) * BOX + HALF, j.astype(F32) * BOX + HALF] + [t.astype(F32) for t in there])
    codes, own_fields, own_factors, right = call(
        prepare_kernel,
        [((24, 128), I32), ((OWN, 8, 128), F32), ((OWN, 128, KEYS), BF16), ((OWN, KEYS, 256), BF16)],
        smem=2,
        args=(pair_count, centre, listed, moved),
    )
    density, press, fields, factors = call(
        density_kernel,
        [((OWN, 128), F32), ((OWN, 128), F32), ((ALL, 8, 128), F32), ((ALL, 128, KEYS), BF16)],
        scratch=[pltpu.VMEM((OWN, 8, 128), F32), pltpu.VMEM((DEPTH[0], 128, 256), F32)],
        smem=2,
        args=(codes, centre, own_fields, own_factors, right, *ghosts),
    )
    presses = around(press[:GT])
    own_pulls, right = call(
        between_kernel,
        [((OWN, 32, 256), BF16), ((OWN, KEYS, 256), BF16)],
        args=(fields, press),
    )
    (accel,) = call(
        accel_kernel,
        [((3, rows), F32)],
        scratch=[
            pltpu.VMEM((ALL, 32, 256), BF16),
            pltpu.VMEM((OWN, 32, 128), F32),
            pltpu.VMEM((DEPTH[1], 128, 256), F32),
            pltpu.VMEM((DEPTH[1], 128, 256), F32),
        ],
        smem=1,
        args=(codes, fields, factors, own_pulls, right, press, *presses),
    )
    return density.reshape(rows), accel


def solution(mesh):
    placed = (
        P(None, ("gx", "gy")),
        P(("gx", "gy")),
        P(("gx", "gy")),
        P(("gx", "gy")),
        P(("gx", "gy"), None),
        P(None, ("gx", "gy")),
        P(("gx", "gy")),
    )
    return jax.shard_map(
        local,
        mesh=mesh,
        in_specs=placed,
        out_specs=(P(("gx", "gy")), P(None, ("gx", "gy"))),
        check_vma=False,
    )
```

```python
import functools
import math

import jax
import jax.numpy as jnp
from jax import lax
from jax.experimental import pallas as pl
from jax.experimental.pallas import tpu as pltpu
from jax.sharding import PartitionSpec as P

F32, BF16, I32 = jnp.float32, jnp.bfloat16, jnp.int32
TILE = 128
OWN = 32
GT = 8
ALL = OWN + 4 * GT
CAP = 16
BOX = 16.0
HALF = 8.0
KEYS = 48
DEPTH = (24, 20)
KERNEL_NORM = 21.0 / (2.0 * math.pi)
GAMMA_LESS = 2.0 / 3.0

NT = (((1,), (1,)), ((), ()))
NN = (((1,), (0,)), ((), ()))


def iota(shape, axis):
    return lax.broadcasted_iota(I32, shape, axis)


def dot(a, b, dims=NN):
    return lax.dot_general(a, b, dims, preferred_element_type=F32)


def pieces(v):
    one = v.astype(BF16).astype(F32)
    rest = v - one
    two = rest.astype(BF16).astype(F32)
    return one, two, rest - two


def first_kernel(count, *refs):
    arguments, out, codes, held, done = refs[:6], refs[6], refs[7], refs[8:14], refs[14]
    copies = [pltpu.make_async_copy(a, b, done.at[k]) for k, (a, b) in enumerate(zip(arguments, held))]
    for copy in copies:
        copy.start()
    for copy in copies:
        copy.wait()
    dispatch(*held[:5], out)
    list_pairs(count, held[5], codes)


def dispatch(pos, mass, smooth, energy, dest, out):
    width = 256
    n = pos.shape[1]
    row = iota((width, width), 0)
    upper = (row < iota((width, width), 1)).astype(F32).astype(BF16)
    ones = jnp.ones((width, width), BF16)
    carry = jnp.zeros((width, width), F32)
    total = jnp.zeros((width, 128), F32)
    ranks = iota((CAP, width), 0)
    for b in range(n // width):
        at = slice(b * width, (b + 1) * width)
        mine = row == dest[:, at]
        hot = jnp.where(mine, 1.0, 0.0)
        hot16 = hot.astype(BF16)
        before = dot(hot16, upper) + carry
        carry = carry + dot(hot16, ones)
        rank = jnp.sum(hot * before, axis=0, keepdims=True).astype(I32)
        sel = ranks == rank
        rows = [pos[0:1, at], pos[1:2, at], pos[2:3, at], mass[:, at], smooth[:, at], energy[:, at]]
        spread = jnp.concatenate(
            [jnp.where(sel, v, 0.0) for v in rows] + [jnp.zeros((2 * CAP, width), F32)], axis=0
        )
        for piece in pieces(spread):
            total = total + dot(hot16, piece.astype(BF16), NT)
    out[...] = total


def list_pairs(count, pairs, out):
    slots = pairs.shape[1]
    target, source = pairs[0:1, :], pairs[1:2, :]
    ghost = (source >= OWN).astype(I32)
    line = jnp.where(iota((1, slots), 1) < count[0], 2 * target + ghost, -1)
    column = source - OWN * ghost
    lines = jnp.where(iota((ALL, slots), 0) == line, 1.0, 0.0).astype(BF16)
    columns = jnp.where(iota((OWN, slots), 0) == column, 1.0, 0.0).astype(BF16)
    times = dot(columns, lines, NT)
    has = jnp.where(times > 0.0, 1.0, 0.0)
    has16 = has.astype(BF16)
    lower = jnp.where(iota((OWN, OWN), 0) > iota((OWN, OWN), 1), 1.0, 0.0).astype(BF16)
    within = dot(lower, has16)
    per_line = dot(jnp.ones((OWN, OWN), BF16), has16)
    la, lb = iota((ALL, ALL), 0), iota((ALL, ALL), 1)

    ahead = jnp.where(la < lb, 1.0, 0.0).astype(BF16)
    lane = iota((OWN, ALL), 1)
    place = within + dot(per_line.astype(BF16), ahead)
    high = jnp.floor(place * (1.0 / 128.0))
    low = (place - 128.0 * high).astype(I32)
    high = jnp.where(has > 0.0, high.astype(I32), -1)
    sub = iota((OWN, ALL), 0)
    code = times * 2048.0 + ((lane // 2) * 64 + sub + (lane % 2) * OWN).astype(F32)
    total = jnp.zeros((48, 128), F32)
    parts = pieces(code)
    for k in range(OWN):
        picked = iota((16, ALL), 0) == high[k : k + 1]
        left = jnp.concatenate([jnp.where(picked, p[k : k + 1], 0.0) for p in parts], axis=0)
        right = jnp.where(iota((128, ALL), 0) == low[k : k + 1], 1.0, 0.0)
        total = total + dot(left.astype(BF16), right.astype(BF16), NT)
    out[0:16] = (total[0:16] + total[16:32] + total[32:48]).astype(I32)
    tally = jnp.sum(per_line[0:1], axis=1, keepdims=True)
    out[16:24] = jnp.broadcast_to(tally, (8, 128)).astype(I32)


def fields_of(block, shift):
    sub, lane = iota((8, 128), 0), iota((8, 128), 1) // CAP
    for bit in (1, 2, 4):
        up = pltpu.roll(pltpu.roll(block, bit, 0), 128 - CAP * bit, 1)
        down = up if bit == 4 else pltpu.roll(pltpu.roll(block, 8 - bit, 0), CAP * bit, 1)
        i, j = (sub // bit) % 2, (lane // bit) % 2
        block = jnp.where(i == j, block, jnp.where(i == 1, up, down))
    block = block - shift
    square = jnp.sum(jnp.where(sub < 3, block * block, 0.0), axis=0, keepdims=True)
    return jnp.where(sub == 6, square, jnp.where(sub == 7, 1.0, block))


def source_factor(v):
    a, b, c = pieces(v)
    return jnp.concatenate([a, a, a, b, b, c], axis=0)


def target_factor(u):
    a, b, c = pieces(u)
    return jnp.concatenate([a, b, c, a, b, a], axis=0)


def coefficients(v):
    sub = iota((8, 128), 0)
    return jnp.where(sub < 3, -2.0 * v, jnp.where(sub == 6, 1.0, jnp.where(sub == 7, v[6:7], 0.0)))


def entry(codes, e):
    code = codes[e >> 7, e & 127]
    return (code >> 6) & (OWN - 1), code & (ALL - 1), code >> 11


def sweep(codes, product, process, buffers):
    turns, depth = len(buffers), buffers[0].shape[0]
    last = OWN * ALL - 1
    count = codes[16, 0]

    def load(e, buffer, k):
        t, s, _ = entry(codes, jnp.minimum(e, last))
        buffer[k] = product(t, s)

    def work(e, buffer, k):
        t, s, times = entry(codes, jnp.minimum(e, last))
        process(t, s, jnp.where(e < count, times, 0), buffer, k)

    for k in range(depth):
        load(k, buffers[0], k)

    def body(i, unused):
        for turn in range(turns):
            for k in range(depth):
                e = (i * turns + turn) * depth + k
                if turns == 1:
                    work(e, buffers[0], k)
                    load(e + depth, buffers[0], k)
                else:
                    load(e + depth, buffers[1 - turn], k)
                    work(e, buffers[turn], k)
        return unused

    lax.fori_loop(0, (count + turns * depth - 1) // (turns * depth), body, 0)


def origin(centre):
    sub = iota((8, 128), 0)
    return jnp.where(sub == 0, centre[0], jnp.where(sub == 1, centre[1], jnp.where(sub == 2, HALF, 0.0)))


def place(tile, block, shift, fields, factors):
    v = fields_of(block, shift)
    fields[tile] = v
    factors[tile] = jnp.transpose(source_factor(v)).astype(BF16)
    return v


def prepare_kernel(centre, listed, moved, codes, fields, factors, right):
    codes[...] = listed[...]
    shift = origin(centre)
    none = jnp.zeros((8, 128), F32)
    weigh = jnp.where(iota((8, 128), 0) == 3, 4.0, 0.0)
    weigh = jnp.concatenate([weigh, none, none, weigh, none, weigh], axis=0).astype(BF16)

    def own(tile, unused):
        v = place(tile, moved[pl.ds(pl.multiple_of(tile * 8, 8), 8)], shift, fields, factors)
        h = v[4:5]
        right[tile, :, 0:128] = target_factor(coefficients(v) * (1.0 / (h * h))).astype(BF16)
        right[tile, :, 128:256] = weigh
        return unused

    lax.fori_loop(0, OWN, own, 0, unroll=8)


def density_kernel(codes, centre, own_fields, own_factors, right, g0, g1, g2, g3, density, press, fields, factors, sums, buffer):
    shift = origin(centre)
    fields[0:OWN] = own_fields[...]
    factors[0:OWN] = own_factors[...]
    sums[...] = jnp.zeros((OWN, 8, 128), F32)
    for k, ghost in enumerate((g0, g1, g2, g3)):
        there = jnp.full((8, 128), centre[2 + k], F32) > 0.0

        def other(tile, unused):
            block = ghost[pl.ds(pl.multiple_of(tile * 8, 8), 8)]
            place(OWN + k * GT + tile, jnp.where(there, block, 0.0), shift, fields, factors)
            return unused

        lax.fori_loop(0, GT, other, 0, unroll=8)

    def product(t, s):
        return dot(factors[s], right[t])

    def process(t, s, times, buffer, k):
        ratio_sq = jnp.maximum(buffer[k, :, 0:128], 1e-30)
        ratio = ratio_sq * lax.rsqrt(ratio_sq)
        falloff = jnp.maximum(1.0 - ratio, 0.0)
        falloff = falloff * falloff
        falloff = falloff * falloff
        term = falloff * (ratio + 0.25) * buffer[k, :, 128:256]
        sums[t] += jnp.sum(term.reshape(16, 8, 128), axis=0) * jnp.full((8, 128), times, I32).astype(F32)

    sweep(codes, product, process, (buffer,))
    total = jnp.sum(sums[...], axis=1)
    h = fields[0:OWN, 4, :]
    result = KERNEL_NORM / (h * h * h) * (total + fields[0:OWN, 3, :])
    density[...] = result
    press[...] = GAMMA_LESS * fields[0:OWN, 5, :] / result


def pull(tile, v, p, pulls):
    sub = iota((8, 128), 0)
    x = jnp.where(sub < 4, pltpu.roll(v, 1, 0), pltpu.roll(v, 5, 0))
    x = jnp.where(sub % 4 == 0, 1.0, x) * v[3:4]
    x = jnp.where(sub < 4, x, x * p)
    both = jnp.concatenate([*pieces(x), jnp.zeros((8, 128), F32)], axis=0).astype(BF16)
    pulls[tile, :, 0:128] = both
    pulls[tile, :, 128:256] = both


def between_kernel(fields, press, pulls, right):
    sub = iota((8, 128), 0)

    def own(tile, unused):
        v = fields[tile]
        pull(tile, v, press[pl.ds(tile, 1)], pulls)
        right[tile, :, 0:128] = target_factor(4.0 * coefficients(v)).astype(BF16)
        h = jnp.where(sub == 4, 1.0, jnp.where(sub == 7, v[4:5], 0.0))
        right[tile, :, 128:256] = target_factor(h).astype(BF16)
        return unused

    lax.fori_loop(0, OWN, own, 0, unroll=8)


def accel_kernel(codes, fields, factors, own_pulls, right, press, p0, p1, p2, p3, accel, pulls, sums, buf0, buf1):
    pulls[0:OWN] = own_pulls[...]
    sums[...] = jnp.zeros((OWN, 32, 128), F32)
    for k, ghost in enumerate((p0, p1, p2, p3)):

        def other(tile, unused):
            pull(OWN + k * GT + tile, fields[OWN + k * GT + tile], ghost[pl.ds(tile, 1)], pulls)
            return unused

        lax.fori_loop(0, GT, other, 0, unroll=8)

    def product(t, s):
        return dot(factors[s], right[t])

    def process(t, s, times, buffer, k):
        dist_sq = jnp.maximum(buffer[k, :, 0:128], 1e-30)
        near = 1.0 / buffer[k, :, 128:256]
        near_sq = near * near
        gap = jnp.maximum(near - dist_sq * lax.rsqrt(dist_sq) * near_sq, 0.0)
        slope = gap * gap * gap * near_sq
        first = slope.astype(BF16)
        second = (slope - first.astype(F32)).astype(BF16)
        both = jnp.concatenate([first, second], axis=0)
        sums[t] += dot(pulls[s], both) * jnp.full((32, 128), times, I32).astype(F32)

    sweep(codes, product, process, (buf0, buf1))

    def finish(tile, unused):
        v = fields[tile]
        s = sums[tile]
        s = s[0:8] + s[8:16] + s[16:24]
        p = press[pl.ds(tile, 1)]
        a = p * (v * s[0:1] - pltpu.roll(s, 7, 0)) + (v * s[4:5] - pltpu.roll(s, 3, 0))
        accel[:, pl.ds(pl.multiple_of(tile * 128, 128), 128)] = a[0:3] * (640.0 * KERNEL_NORM)
        return unused

    lax.fori_loop(0, OWN, finish, 0)


def call(kernel, shapes, scratch=(), smem=0, anywhere=0, args=(), limit=40):
    specs = [pl.BlockSpec(memory_space=pltpu.SMEM)] * smem
    specs += [pl.BlockSpec(memory_space=pl.ANY)] * anywhere
    specs += [pl.BlockSpec(memory_space=pltpu.VMEM)] * (len(args) - smem - anywhere)
    return pl.pallas_call(
        kernel,
        out_shape=[jax.ShapeDtypeStruct(s, d) for s, d in shapes],
        in_specs=specs,
        out_specs=[pl.BlockSpec(memory_space=pltpu.VMEM)] * len(shapes),
        scratch_shapes=list(scratch),
        compiler_params=pltpu.CompilerParams(vmem_limit_bytes=limit * 2**20),
    )(*args)


def around(edge):
    taken = []
    for axis in ("gx", "gy"):
        count = lax.axis_size(axis)
        forward = [(i, (i + 1) % count) for i in range(count)]
        taken.append(lax.ppermute(edge, axis, forward))
        taken.append(lax.ppermute(edge, axis, [(b, a) for a, b in forward]))
    return taken


def local(positions, mass, smoothing, energy, destination, pairs, pair_count):
    rows = mass.shape[0]
    flat = [a.reshape(1, rows) for a in (mass, smoothing, energy, destination)]
    given = (positions, *flat, pairs)
    outgoing, listed = call(
        first_kernel,
        [((256, 128), F32), ((24, 128), I32)],
        scratch=[pltpu.VMEM(a.shape, a.dtype) for a in given] + [pltpu.SemaphoreType.DMA((len(given),))],
        smem=1,
        anywhere=len(given),
        args=(pair_count, *given),
        limit=60,
    )
    moved = lax.all_to_all(outgoing, ("gx", "gy"), split_axis=0, concat_axis=0, tiled=True)
    ghosts = around(moved[: GT * 8])
    i, j = lax.axis_index("gx"), lax.axis_index("gy")
    there = [i > 0, i < lax.axis_size("gx") - 1, j > 0, j < lax.axis_size("gy") - 1]
    centre = jnp.stack([i.astype(F32) * BOX + HALF, j.astype(F32) * BOX + HALF] + [t.astype(F32) for t in there])
    codes, own_fields, own_factors, right = call(
        prepare_kernel,
        [((24, 128), I32), ((OWN, 8, 128), F32), ((OWN, 128, KEYS), BF16), ((OWN, KEYS, 256), BF16)],
        smem=1,
        args=(centre, listed, moved),
    )
    density, press, fields, factors = call(
        density_kernel,
        [((OWN, 128), F32), ((OWN, 128), F32), ((ALL, 8, 128), F32), ((ALL, 128, KEYS), BF16)],
        scratch=[pltpu.VMEM((OWN, 8, 128), F32), pltpu.VMEM((DEPTH[0], 128, 256), F32)],
        smem=2,
        args=(codes, centre, own_fields, own_factors, right, *ghosts),
    )
    presses = around(press[:GT])
    own_pulls, right = call(
        between_kernel,
        [((OWN, 32, 256), BF16), ((OWN, KEYS, 256), BF16)],
        args=(fields, press),
    )
    (accel,) = call(
        accel_kernel,
        [((3, rows), F32)],
        scratch=[
            pltpu.VMEM((ALL, 32, 256), BF16),
            pltpu.VMEM((OWN, 32, 128), F32),
            pltpu.VMEM((DEPTH[1], 128, 256), F32),
            pltpu.VMEM((DEPTH[1], 128, 256), F32),
        ],
        smem=1,
        args=(codes, fields, factors, own_pulls, right, press, *presses),
    )
    return density.reshape(rows), accel


def solution(mesh):
    placed = (
        P(None, ("gx", "gy")),
        P(("gx", "gy")),
        P(("gx", "gy")),
        P(("gx", "gy")),
        P(("gx", "gy"), None),
        P(None, ("gx", "gy")),
        P(("gx", "gy")),
    )
    return jax.shard_map(
        local,
        mesh=mesh,
        in_specs=placed,
        out_specs=(P(("gx", "gy")), P(None, ("gx", "gy"))),
        check_vma=False,
    )
```

```python
import functools
import math

import jax
import jax.numpy as jnp
from jax import lax
from jax.experimental import pallas as pl
from jax.experimental.pallas import tpu as pltpu
from jax.sharding import PartitionSpec as P

F32, BF16, I32 = jnp.float32, jnp.bfloat16, jnp.int32
TILE = 128
OWN = 32
GT = 8
ALL = OWN + 4 * GT
CAP = 16
BOX = 16.0
HALF = 8.0
KEYS = 48
DEPTH = (24, 20)
KERNEL_NORM = 21.0 / (2.0 * math.pi)
GAMMA_LESS = 2.0 / 3.0

NT = (((1,), (1,)), ((), ()))
NN = (((1,), (0,)), ((), ()))


def iota(shape, axis):
    return lax.broadcasted_iota(I32, shape, axis)


def dot(a, b, dims=NN):
    return lax.dot_general(a, b, dims, preferred_element_type=F32)


def pieces(v):
    one = v.astype(BF16).astype(F32)
    rest = v - one
    two = rest.astype(BF16).astype(F32)
    return one, two, rest - two


def first_kernel(count, *refs):
    arguments, out, codes, held, done = refs[:6], refs[6], refs[7], refs[8:14], refs[14]
    copies = [pltpu.make_async_copy(a, b, done.at[k]) for k, (a, b) in enumerate(zip(arguments, held))]
    for copy in copies:
        copy.start()
    for copy in copies:
        copy.wait()
    dispatch(*held[:5], out)
    list_pairs(count, held[5], codes)


def dispatch(pos, mass, smooth, energy, dest, out):
    width = 256
    n = pos.shape[1]
    row = iota((width, width), 0)
    upper = (row < iota((width, width), 1)).astype(F32).astype(BF16)
    ones = jnp.ones((width, width), BF16)
    carry = jnp.zeros((width, width), F32)
    total = jnp.zeros((width, 6 * CAP), F32)
    ranks = iota((CAP, width), 0)
    for b in range(n // width):
        at = slice(b * width, (b + 1) * width)
        mine = row == dest[:, at]
        hot = jnp.where(mine, 1.0, 0.0)
        hot16 = hot.astype(BF16)
        before = dot(hot16, upper) + carry
        carry = carry + dot(hot16, ones)
        rank = jnp.sum(hot * before, axis=0, keepdims=True).astype(I32)
        sel = ranks == rank
        rows = [pos[0:1, at], pos[1:2, at], pos[2:3, at], mass[:, at], smooth[:, at], energy[:, at]]
        spread = jnp.concatenate([jnp.where(sel, v, 0.0) for v in rows], axis=0)
        for piece in pieces(spread):
            total = total + dot(hot16, piece.astype(BF16), NT)
    out[:, 0 : 6 * CAP] = total
    out[:, 6 * CAP : 128] = jnp.zeros((width, 128 - 6 * CAP), F32)


def list_pairs(count, pairs, out):
    slots = pairs.shape[1]
    target, source = pairs[0:1, :], pairs[1:2, :]
    ghost = (source >= OWN).astype(I32)
    line = jnp.where(iota((1, slots), 1) < count[0], 2 * target + ghost, -1)
    column = source - OWN * ghost
    lines = jnp.where(iota((ALL, slots), 0) == line, 1.0, 0.0).astype(BF16)
    columns = jnp.where(iota((OWN, slots), 0) == column, 1.0, 0.0).astype(BF16)
    times = dot(columns, lines, NT)
    has = jnp.where(times > 0.0, 1.0, 0.0)
    has16 = has.astype(BF16)
    lower = jnp.where(iota((OWN, OWN), 0) > iota((OWN, OWN), 1), 1.0, 0.0).astype(BF16)
    within = dot(lower, has16)
    per_line = dot(jnp.ones((OWN, OWN), BF16), has16)
    la, lb = iota((ALL, ALL), 0), iota((ALL, ALL), 1)

    ahead = jnp.where(la < lb, 1.0, 0.0).astype(BF16)
    lane = iota((OWN, ALL), 1)
    place = within + dot(per_line.astype(BF16), ahead)
    high = jnp.floor(place * (1.0 / 128.0))
    low = (place - 128.0 * high).astype(I32)
    high = jnp.where(has > 0.0, high.astype(I32), -1)
    sub = iota((OWN, ALL), 0)
    code = times * 2048.0 + ((lane // 2) * 64 + sub + (lane % 2) * OWN).astype(F32)
    total = jnp.zeros((48, 128), F32)
    parts = pieces(code)
    for k in range(OWN):
        picked = iota((16, ALL), 0) == high[k : k + 1]
        left = jnp.concatenate([jnp.where(picked, p[k : k + 1], 0.0) for p in parts], axis=0)
        right = jnp.where(iota((128, ALL), 0) == low[k : k + 1], 1.0, 0.0)
        total = total + dot(left.astype(BF16), right.astype(BF16), NT)
    out[0:16] = (total[0:16] + total[16:32] + total[32:48]).astype(I32)
    tally = jnp.sum(per_line[0:1], axis=1, keepdims=True)
    out[16:24] = jnp.broadcast_to(tally, (8, 128)).astype(I32)


def fields_of(block, shift):
    sub, lane = iota((8, 128), 0), iota((8, 128), 1) // CAP
    for bit in (1, 2, 4):
        up = pltpu.roll(pltpu.roll(block, bit, 0), 128 - CAP * bit, 1)
        down = up if bit == 4 else pltpu.roll(pltpu.roll(block, 8 - bit, 0), CAP * bit, 1)
        i, j = (sub // bit) % 2, (lane // bit) % 2
        block = jnp.where(i == j, block, jnp.where(i == 1, up, down))
    block = block - shift
    square = jnp.sum(jnp.where(sub < 3, block * block, 0.0), axis=0, keepdims=True)
    return jnp.where(sub == 6, square, jnp.where(sub == 7, 1.0, block))


def source_factor(v):
    a, b, c = pieces(v)
    return jnp.concatenate([a, a, a, b, b, c], axis=0)


def target_factor(u):
    a, b, c = pieces(u)
    return jnp.concatenate([a, b, c, a, b, a], axis=0)


def coefficients(v):
    sub = iota((8, 128), 0)
    return jnp.where(sub < 3, -2.0 * v, jnp.where(sub == 6, 1.0, jnp.where(sub == 7, v[6:7], 0.0)))


def entry(codes, e):
    code = codes[e >> 7, e & 127]
    return (code >> 6) & (OWN - 1), code & (ALL - 1), code >> 11


def sweep(codes, product, process, buffers):
    turns, depth = len(buffers), buffers[0].shape[0]
    last = OWN * ALL - 1
    count = codes[16, 0]

    def load(e, buffer, k):
        t, s, _ = entry(codes, jnp.minimum(e, last))
        buffer[k] = product(t, s)

    def work(e, buffer, k):
        t, s, times = entry(codes, jnp.minimum(e, last))
        process(t, s, jnp.where(e < count, times, 0), buffer, k)

    for k in range(depth):
        load(k, buffers[0], k)

    def body(i, unused):
        for turn in range(turns):
            for k in range(depth):
                e = (i * turns + turn) * depth + k
                if turns == 1:
                    work(e, buffers[0], k)
                    load(e + depth, buffers[0], k)
                else:
                    load(e + depth, buffers[1 - turn], k)
                    work(e, buffers[turn], k)
        return unused

    lax.fori_loop(0, (count + turns * depth - 1) // (turns * depth), body, 0)


def origin(centre):
    sub = iota((8, 128), 0)
    return jnp.where(sub == 0, centre[0], jnp.where(sub == 1, centre[1], jnp.where(sub == 2, HALF, 0.0)))


def place(tile, block, shift, fields, factors):
    v = fields_of(block, shift)
    fields[tile] = v
    factors[tile] = jnp.transpose(source_factor(v)).astype(BF16)
    return v


def prepare_kernel(centre, listed, moved, codes, fields, factors, right):
    codes[...] = listed[...]
    shift = origin(centre)
    none = jnp.zeros((8, 128), F32)
    weigh = jnp.where(iota((8, 128), 0) == 3, 4.0, 0.0)
    weigh = jnp.concatenate([weigh, none, none, weigh, none, weigh], axis=0).astype(BF16)

    def own(tile, unused):
        v = place(tile, moved[pl.ds(pl.multiple_of(tile * 8, 8), 8)], shift, fields, factors)
        h = v[4:5]
        right[tile, :, 0:128] = target_factor(coefficients(v) * (1.0 / (h * h))).astype(BF16)
        right[tile, :, 128:256] = weigh
        return unused

    lax.fori_loop(0, OWN, own, 0, unroll=8)


def density_kernel(codes, centre, own_fields, own_factors, right, g0, g1, g2, g3, density, press, fields, factors, sums, buffer):
    shift = origin(centre)
    fields[0:OWN] = own_fields[...]
    factors[0:OWN] = own_factors[...]
    sums[...] = jnp.zeros((OWN, 8, 128), F32)
    for k, ghost in enumerate((g0, g1, g2, g3)):
        there = jnp.full((8, 128), centre[2 + k], F32) > 0.0

        def other(tile, unused):
            block = ghost[pl.ds(pl.multiple_of(tile * 8, 8), 8)]
            place(OWN + k * GT + tile, jnp.where(there, block, 0.0), shift, fields, factors)
            return unused

        lax.fori_loop(0, GT, other, 0, unroll=8)

    def product(t, s):
        return dot(factors[s], right[t])

    def process(t, s, times, buffer, k):
        ratio_sq = jnp.maximum(buffer[k, :, 0:128], 1e-30)
        ratio = ratio_sq * lax.rsqrt(ratio_sq)
        falloff = jnp.maximum(1.0 - ratio, 0.0)
        falloff = falloff * falloff
        falloff = falloff * falloff
        term = falloff * (ratio + 0.25) * buffer[k, :, 128:256]
        sums[t] += jnp.sum(term.reshape(16, 8, 128), axis=0) * jnp.full((8, 128), times, I32).astype(F32)

    sweep(codes, product, process, (buffer,))
    total = jnp.sum(sums[...], axis=1)
    h = fields[0:OWN, 4, :]
    result = KERNEL_NORM / (h * h * h) * (total + fields[0:OWN, 3, :])
    density[...] = result
    press[...] = GAMMA_LESS * fields[0:OWN, 5, :] / result


def pull(tile, v, p, pulls):
    sub = iota((8, 128), 0)
    x = jnp.where(sub < 4, pltpu.roll(v, 1, 0), pltpu.roll(v, 5, 0))
    x = jnp.where(sub % 4 == 0, 1.0, x) * v[3:4]
    x = jnp.where(sub < 4, x, x * p)
    both = jnp.concatenate([*pieces(x), jnp.zeros((8, 128), F32)], axis=0).astype(BF16)
    pulls[tile, :, 0:128] = both
    pulls[tile, :, 128:256] = both


def between_kernel(fields, press, pulls, right):
    sub = iota((8, 128), 0)

    def own(tile, unused):
        v = fields[tile]
        pull(tile, v, press[pl.ds(tile, 1)], pulls)
        right[tile, :, 0:128] = target_factor(4.0 * coefficients(v)).astype(BF16)
        h = jnp.where(sub == 4, 1.0, jnp.where(sub == 7, v[4:5], 0.0))
        right[tile, :, 128:256] = target_factor(h).astype(BF16)
        return unused

    lax.fori_loop(0, OWN, own, 0, unroll=8)


def accel_kernel(codes, fields, factors, own_pulls, right, press, p0, p1, p2, p3, accel, pulls, sums, buf0, buf1):
    pulls[0:OWN] = own_pulls[...]
    sums[...] = jnp.zeros((OWN, 32, 128), F32)
    for k, ghost in enumerate((p0, p1, p2, p3)):

        def other(tile, unused):
            pull(OWN + k * GT + tile, fields[OWN + k * GT + tile], ghost[pl.ds(tile, 1)], pulls)
            return unused

        lax.fori_loop(0, GT, other, 0, unroll=8)

    def product(t, s):
        return dot(factors[s], right[t])

    def process(t, s, times, buffer, k):
        dist_sq = jnp.maximum(buffer[k, :, 0:128], 1e-30)
        near = 1.0 / buffer[k, :, 128:256]
        near_sq = near * near
        gap = jnp.maximum(near - dist_sq * lax.rsqrt(dist_sq) * near_sq, 0.0)
        slope = gap * gap * gap * near_sq
        first = slope.astype(BF16)
        second = (slope - first.astype(F32)).astype(BF16)
        both = jnp.concatenate([first, second], axis=0)
        sums[t] += dot(pulls[s], both) * jnp.full((32, 128), times, I32).astype(F32)

    sweep(codes, product, process, (buf0, buf1))

    def finish(tile, unused):
        v = fields[tile]
        s = sums[tile]
        s = s[0:8] + s[8:16] + s[16:24]
        p = press[pl.ds(tile, 1)]
        a = p * (v * s[0:1] - pltpu.roll(s, 7, 0)) + (v * s[4:5] - pltpu.roll(s, 3, 0))
        accel[:, pl.ds(pl.multiple_of(tile * 128, 128), 128)] = a[0:3] * (640.0 * KERNEL_NORM)
        return unused

    lax.fori_loop(0, OWN, finish, 0)


def call(kernel, shapes, scratch=(), smem=0, anywhere=0, args=(), limit=40):
    specs = [pl.BlockSpec(memory_space=pltpu.SMEM)] * smem
    specs += [pl.BlockSpec(memory_space=pl.ANY)] * anywhere
    specs += [pl.BlockSpec(memory_space=pltpu.VMEM)] * (len(args) - smem - anywhere)
    return pl.pallas_call(
        kernel,
        out_shape=[jax.ShapeDtypeStruct(s, d) for s, d in shapes],
        in_specs=specs,
        out_specs=[pl.BlockSpec(memory_space=pltpu.VMEM)] * len(shapes),
        scratch_shapes=list(scratch),
        compiler_params=pltpu.CompilerParams(vmem_limit_bytes=limit * 2**20),
    )(*args)


def around(edge):
    taken = []
    for axis in ("gx", "gy"):
        count = lax.axis_size(axis)
        forward = [(i, (i + 1) % count) for i in range(count)]
        taken.append(lax.ppermute(edge, axis, forward))
        taken.append(lax.ppermute(edge, axis, [(b, a) for a, b in forward]))
    return taken


def local(positions, mass, smoothing, energy, destination, pairs, pair_count):
    rows = mass.shape[0]
    flat = [a.reshape(1, rows) for a in (mass, smoothing, energy, destination)]
    given = (positions, *flat, pairs)
    outgoing, listed = call(
        first_kernel,
        [((256, 128), F32), ((24, 128), I32)],
        scratch=[pltpu.VMEM(a.shape, a.dtype) for a in given] + [pltpu.SemaphoreType.DMA((len(given),))],
        smem=1,
        anywhere=len(given),
        args=(pair_count, *given),
        limit=60,
    )
    moved = lax.all_to_all(outgoing, ("gx", "gy"), split_axis=0, concat_axis=0, tiled=True)
    ghosts = around(moved[: GT * 8])
    i, j = lax.axis_index("gx"), lax.axis_index("gy")
    there = [i > 0, i < lax.axis_size("gx") - 1, j > 0, j < lax.axis_size("gy") - 1]
    centre = jnp.stack([i.astype(F32) * BOX + HALF, j.astype(F32) * BOX + HALF] + [t.astype(F32) for t in there])
    codes, own_fields, own_factors, right = call(
        prepare_kernel,
        [((24, 128), I32), ((OWN, 8, 128), F32), ((OWN, 128, KEYS), BF16), ((OWN, KEYS, 256), BF16)],
        smem=1,
        args=(centre, listed, moved),
    )
    density, press, fields, factors = call(
        density_kernel,
        [((OWN, 128), F32), ((OWN, 128), F32), ((ALL, 8, 128), F32), ((ALL, 128, KEYS), BF16)],
        scratch=[pltpu.VMEM((OWN, 8, 128), F32), pltpu.VMEM((DEPTH[0], 128, 256), F32)],
        smem=2,
        args=(codes, centre, own_fields, own_factors, right, *ghosts),
    )
    presses = around(press[:GT])
    own_pulls, right = call(
        between_kernel,
        [((OWN, 32, 256), BF16), ((OWN, KEYS, 256), BF16)],
        args=(fields, press),
    )
    (accel,) = call(
        accel_kernel,
        [((3, rows), F32)],
        scratch=[
            pltpu.VMEM((ALL, 32, 256), BF16),
            pltpu.VMEM((OWN, 32, 128), F32),
            pltpu.VMEM((DEPTH[1], 128, 256), F32),
            pltpu.VMEM((DEPTH[1], 128, 256), F32),
        ],
        smem=1,
        args=(codes, fields, factors, own_pulls, right, press, *presses),
    )
    return density.reshape(rows), accel


def solution(mesh):
    placed = (
        P(None, ("gx", "gy")),
        P(("gx", "gy")),
        P(("gx", "gy")),
        P(("gx", "gy")),
        P(("gx", "gy"), None),
        P(None, ("gx", "gy")),
        P(("gx", "gy")),
    )
    return jax.shard_map(
        local,
        mesh=mesh,
        in_specs=placed,
        out_specs=(P(("gx", "gy")), P(None, ("gx", "gy"))),
        check_vma=False,
    )
```
